32 devices in a mesh: seq: 8 (over y, x, core), chan: 4 (over z).
Axes of the slice: x: 2, y: 2, z: 4, core: 2. Of those that a mesh axis runs over, the one named last changes fastest.
Arguments:
- tokens: int32 [2048], P('seq'), may hold values from 0 to 511
- embedding: bfloat16 [512, 4096], P(None, 'chan'), may hold values from -6 to 6
- norm_gain: float32 [4096], replicated, may hold values from 0.5 to 1.5
- in_weight: bfloat16 [4096, 3, 4096], P(None, None, 'chan'), may hold values from -0.09375 to 0.09375
- short_filter: float32 [3, 3, 4096], P(None, None, 'chan'), may hold values from -3 to 3
- decay_rate: float32 [16, 4096], P(None, 'chan'), may hold values from 9.765625e-06 to 0.025, as said below
- residue: float32 [16, 4096], P(None, 'chan'), may hold values from -0.06 to 0.06
- skip_gain: float32 [4096], P('chan'), may hold values from -4 to 4
- out_weight: bfloat16 [4096, 4096], P('chan'), may hold values from -0.125 to 0.125
Outputs:
- block_out: bfloat16 [2048, 4096], P('seq', 'chan')
The draws below stay inside these ranges and needn't reach their ends.
Inputs may be any that keep to these rules, and one draw needn't show every extreme that they name: `decay_rate`: positive rates.
All inputs are finite; a program needn't handle non-finite values.
Results may differ from the reference program's by a relative error of at most 0.0091.
Values may be sent and summed in bfloat16 or wider, within the bound.
A program may use at most 256 MiB of HBM per device.

```python
import math
import jax
import jax.numpy as jnp
import numpy as np
from jax import lax

D = 4096
VOCAB = 512
MODES = 16
FEAT = 3
BLK = 128
TOKENS = 2048


def draw_decay_rate(key, part):
    key_slow = jax.random.fold_in(key, 11)
    low_log = math.log(0.02 / TOKENS)
    high_log = math.log(0.025)
    logs = jax.random.uniform(key_slow, (MODES, D), jnp.float32, low_log, high_log)
    return jnp.exp(logs).astype(jnp.float32)


def touch_ends(drawn, stream_key, low, top_value):
    longest = drawn.shape.index(max(drawn.shape))
    spots = []
    for shift in (0, 1):
        where = [jax.random.randint(jax.random.fold_in(stream_key, axis), (), 0, length) for axis, length in enumerate(drawn.shape)]
        where[longest] = (where[longest] + shift) % drawn.shape[longest]
        spots.append(tuple(where))
    return drawn.at[spots[0]].set(low).at[spots[1]].set(top_value)


def raised(drawn, stream_key, source, target, blocks, factor):
    def block_of(axis_at):
        return (jnp.arange(drawn.shape[axis_at]) // (drawn.shape[axis_at] // blocks)).reshape((-1,) + (1,) * (drawn.ndim - 1 - axis_at))

    one_side = jax.random.permutation(stream_key, blocks)[block_of(target)]
    far = (block_of(target) + blocks // 2) % blocks
    return jnp.where((block_of(source) == one_side) | (block_of(source) == far), factor * drawn, drawn)


def levels(own_key, shape, cuts, least, top_value):
    level, own = 1.0, jax.random.fold_in(own_key, 6)
    for dim, blocks in cuts:
        steps = jnp.exp(jax.random.uniform(jax.random.fold_in(own, dim), (blocks,), jnp.float32, least / len(cuts), top_value / len(cuts)))
        level = level * jnp.repeat(steps, shape[dim] // blocks).reshape([-1 if axis == dim else 1 for axis in range(len(shape))])
    return level


def rank_table(amount, slope):
    weights = [(1 << 20) // math.isqrt(rank ** slope) + 1 for rank in range(1, amount + 1)]
    width = 1 + sum(weights) // (1 << 30)
    return np.cumsum(np.array([max(1, weight // width) for weight in weights]))


def ranked(key, dims, count, lean):
    table = rank_table(count, lean)
    pick = jax.random.randint(jax.random.fold_in(key, 1), dims, 0, int(table[count - 1]))
    standing = jnp.searchsorted(jnp.asarray(table, jnp.int32), pick, side="right")
    return jax.random.permutation(jax.random.fold_in(key, 2), count)[standing].astype(jnp.int32)


def noise(key, shape, spread, most, cuts=(), held_as=jnp.bfloat16):
    values = jax.random.normal(key, shape, jnp.float32) * spread
    if len(cuts) > 0:
        values = levels(key, shape, cuts, -0.22, 0.18) * values
    return jnp.clip(values, min=-most, max=most).astype(held_as)


def noise_with(own_key, extent, spread, bound, pieces, heavy, kind=jnp.bfloat16):
    entries = spread * jax.random.normal(own_key, extent, jnp.float32)
    if pieces:
        entries = entries * levels(own_key, extent, pieces, -0.22, 0.18)
    return jnp.clip(raised(entries, jax.random.fold_in(own_key, 3), *heavy), -bound, bound).astype(kind)


def setup_inputs(seed: int = 0) -> dict:
    arg_keys = jax.random.split(jax.random.key(seed), 10)
    tokens = touch_ends(ranked(arg_keys[0], (TOKENS,), VOCAB, 2), jax.random.fold_in(arg_keys[0], 3), 0, VOCAB - 1).astype(jnp.int32)
    embedding = noise(arg_keys[1], (VOCAB, D), 1.0, 6.0, ((1, 4),))
    norm_gain = jnp.clip(1.0 + 0.1 * jax.random.normal(arg_keys[2], (D,), jnp.float32), 0.5, 1.5)
    in_weight = noise(arg_keys[3], (D, 3, D), D ** -0.5, 0.09375, ((2, 4),))
    short_filter = noise(arg_keys[4], (FEAT, 3, D), 0.6, 3.0, ((2, 4),), jnp.float32)
    decay_rate = draw_decay_rate(jax.random.fold_in(arg_keys[9], 71), 0)
    residue = noise(arg_keys[6], (MODES, D), 0.01, 0.06, ((1, 4),), jnp.float32)
    skip_gain = noise(arg_keys[7], (D,), 1.0, 4.0, ((0, 4),), jnp.float32)
    out_weight = noise_with(arg_keys[8], (D, D), D ** -0.5, 0.125, ((0, 4),), (0, 1, 4, 2.0))
    return dict(tokens=tokens, embedding=embedding, norm_gain=norm_gain, in_weight=in_weight, short_filter=short_filter, decay_rate=decay_rate, residue=residue, skip_gain=skip_gain, out_weight=out_weight)


def modal_filter(driven, decay_rate, residue):
    steps_f = jnp.arange(BLK, dtype=jnp.float32)
    lag_table = jnp.arange(BLK)[:, None] - jnp.arange(BLK)[None, :]
    causal = lag_table >= 0
    impulse = lax.optimization_barrier(jnp.sum(residue[:, None, :] * jnp.exp(-decay_rate[:, None, :] * steps_f[None, :, None]), axis=0))
    toeplitz = jnp.where(causal[:, :, None], impulse[jnp.clip(lag_table, 0, BLK - 1)], 0.0)
    w_end = jnp.exp(-decay_rate[:, None, :] * (BLK - 1 - steps_f)[None, :, None])
    r_next = residue[:, None, :] * jnp.exp(-decay_rate[:, None, :] * (steps_f + 1.0)[None, :, None])
    block_decay = jnp.exp(-decay_rate * BLK)
    blocks = driven.reshape(TOKENS // BLK, BLK, D)

    def advance(state, block):
        result = jnp.einsum('ijc,jc->ic', toeplitz, block, precision=lax.Precision.HIGHEST)
        result = result + jnp.einsum('njc,nc->jc', r_next, state, precision=lax.Precision.HIGHEST)
        state = block_decay * state + jnp.einsum('njc,jc->nc', w_end, block, precision=lax.Precision.HIGHEST)
        return (state, result)
    _, results = lax.scan(advance, jnp.zeros((MODES, D), jnp.float32), blocks)
    return results.reshape(TOKENS, D)

def reference(tokens, embedding, norm_gain, in_weight, short_filter, decay_rate, residue, skip_gain, out_weight):
    stream = embedding[tokens]
    stream_f = stream.astype(jnp.float32)
    scale = lax.rsqrt(lax.optimization_barrier(jnp.mean(stream_f * stream_f, axis=1, keepdims=True)) + 1e-06)
    normed = (stream_f * scale * norm_gain[None, :]).astype(jnp.bfloat16)
    proj = jnp.dot(normed, in_weight.reshape(D, 3 * D), preferred_element_type=jnp.float32)
    proj = proj.astype(jnp.bfloat16).reshape(TOKENS, 3, D)
    padded = jnp.concatenate([jnp.zeros((FEAT - 1, 3, D), jnp.bfloat16), proj], axis=0).astype(jnp.float32)
    feat = short_filter[0][None] * padded[FEAT - 1:FEAT - 1 + TOKENS]
    for offset in range(1, FEAT):
        feat = feat + short_filter[offset][None] * padded[FEAT - 1 - offset:FEAT - 1 - offset + TOKENS]
    feat = feat.astype(jnp.bfloat16)
    query = feat[:, 0].astype(jnp.float32)
    driven = feat[:, 1].astype(jnp.float32) * feat[:, 2].astype(jnp.float32)
    long_out = modal_filter(driven, decay_rate, residue) + skip_gain[None, :] * driven
    hidden = (query * long_out).astype(jnp.bfloat16)
    mixed = jnp.dot(hidden, out_weight, preferred_element_type=jnp.float32)
    return (stream_f + mixed).astype(jnp.bfloat16)
```

```python
import functools

import jax
import jax.numpy as jnp
from jax import lax
from jax.experimental import pallas as pl
from jax.experimental.pallas import tpu as pltpu
from jax.sharding import PartitionSpec as P

FEAT = 3
LANES = 128
SEGS = 8
MESH = pl.DeviceIdType.MESH


def block_kernel(
    seq_size,
    chan_size,
    proj_ref,
    stream_ref,
    filter_ref,
    decay_ref,
    residue_ref,
    skip_ref,
    weight_ref,
    out_ref,
    weight_buf,
    rim_out,
    rim_in,
    padded,
    query_buf,
    driven_buf,
    seg_ends,
    own_end,
    all_ends,
    incoming,
    seg_starts,
    hidden_f,
    hidden,
    part,
    sums_out,
    sums_in,
    weight_sem,
    rim_sem,
    end_send_sem,
    end_recv_sem,
    sum_send_sem,
    sum_recv_sem,
):
    place = lax.axis_index("seq")
    shard = lax.axis_index("chan")
    rows, channels = stream_ref.shape
    modes = decay_ref.shape[0]
    groups = channels // LANES
    seg = rows // SEGS

    weight_copies = [
        pltpu.make_async_copy(
            weight_ref.at[:, pl.ds(d * channels, channels)], weight_buf.at[d], weight_sem.at[d]
        )
        for d in range(chan_size)
    ]
    for copy in weight_copies:
        copy.start()

    barrier = pltpu.get_barrier_semaphore()
    for k in range(1, seq_size):
        pl.semaphore_signal(
            barrier, 1, device_id={"seq": lax.rem(place + k, seq_size)}, device_id_type=MESH
        )
    for k in range(1, chan_size):
        pl.semaphore_signal(
            barrier, 1, device_id={"chan": lax.rem(shard + k, chan_size)}, device_id_type=MESH
        )
    for j in range(FEAT):
        rim_out[j] = proj_ref[j, rows - 16 :, :].astype(jnp.float32)[8:]
    pl.semaphore_wait(barrier, seq_size - 1 + chan_size - 1)

    rim_copy = pltpu.make_async_remote_copy(
        src_ref=rim_out,
        dst_ref=rim_in,
        send_sem=rim_sem.at[0],
        recv_sem=rim_sem.at[1],
        device_id={"seq": lax.rem(place + 1, seq_size)},
        device_id_type=MESH,
    )
    rim_copy.start()
    rim_copy.wait()
    keep = (place > 0).astype(jnp.float32)

    def spread(value):
        return jnp.broadcast_to(value[:, None, :], (value.shape[0], SEGS, LANES))

    def first_pass(g, carry):
        lanes = pl.ds(pl.multiple_of(g * LANES, LANES), LANES)
        feat = []
        for j in range(FEAT):
            now = proj_ref[j, :, lanes].astype(jnp.float32)
            padded[j, 8:, :] = now
            padded[j, :8, :] = rim_in[j, :, lanes] * keep
            total = filter_ref[j : j + 1, lanes] * now
            for offset in range(1, FEAT):
                row = offset * FEAT + j
                total = total + filter_ref[row : row + 1, lanes] * padded[j, pl.ds(8 - offset, rows), :]
            feat.append(total.astype(jnp.bfloat16).astype(jnp.float32))
        query_buf[g] = feat[0]
        driven_buf[g] = feat[1] * feat[2]
        decay = decay_ref[:, lanes]
        lam = spread(jnp.exp(-decay))

        def step(i, state):
            x = driven_buf[g, pl.ds(i, SEGS, stride=seg), :]
            return lam * state + x[None]

        state = lax.fori_loop(
            0, seg, step, jnp.zeros((modes, SEGS, LANES), jnp.float32), unroll=8
        )
        seg_ends[g] = state
        lam_seg = jnp.exp(-decay * seg)
        end = state[:, 0, :]
        for s in range(1, SEGS):
            end = lam_seg * end + state[:, s, :]
        own_end[:, lanes] = end
        return carry

    lax.fori_loop(0, groups, first_pass, 0)

    def end_copy(to, source):
        return pltpu.make_async_remote_copy(
            src_ref=own_end,
            dst_ref=all_ends.at[source],
            send_sem=end_send_sem.at[to],
            recv_sem=end_recv_sem.at[source],
            device_id={"seq": to},
            device_id_type=MESH,
        )

    for k in range(1, seq_size):
        end_copy(lax.rem(place + k, seq_size), place).start()
    for k in range(1, seq_size):
        peer = lax.rem(place + k, seq_size)
        end_copy(peer, place).wait_send()
        end_copy(peer, peer).wait_recv()
    all_ends[place] = own_end[...]

    span = jnp.exp(-decay_ref[...] * rows)
    state = jnp.zeros((modes, channels), jnp.float32)
    for p in range(seq_size - 1):
        state = jnp.where(p < place, span * state + all_ends[p], state)
    incoming[...] = state

    def second_pass(g, carry):
        lanes = pl.ds(pl.multiple_of(g * LANES, LANES), LANES)
        decay = decay_ref[:, lanes]
        lam_seg = jnp.exp(-decay * seg)
        start = incoming[:, lanes]
        for s in range(SEGS):
            seg_starts[:, s, :] = start
            start = lam_seg * start + seg_ends[g, :, s, :]
        lam = spread(jnp.exp(-decay))
        gain = spread(residue_ref[:, lanes])
        skip = jnp.broadcast_to(skip_ref[:, lanes], (SEGS, LANES))

        def step(i, state):
            at = pl.ds(i, SEGS, stride=seg)
            x = driven_buf[g, at, :]
            state = lam * state + x[None]
            long = jnp.sum(gain * state, axis=0) + skip * x
            hidden_f[at, :] = query_buf[g, at, :] * long
            return state

        lax.fori_loop(0, seg, step, seg_starts[...], unroll=8)
        hidden[:, lanes] = hidden_f[...].astype(jnp.bfloat16)
        return carry

    lax.fori_loop(0, groups, second_pass, 0)
    for copy in weight_copies:
        copy.wait()

    tile = min(256, channels)

    def project(dest):
        def one(t, carry):
            cols = pl.ds(pl.multiple_of(t * tile, tile), tile)
            part[:, cols] = jnp.dot(
                hidden[...], weight_buf[dest, :, cols], preferred_element_type=jnp.float32
            )
            return carry

        lax.fori_loop(0, channels // tile, one, 0)

    def sum_copy(way, dest, to):
        return pltpu.make_async_remote_copy(
            src_ref=sums_out.at[way, dest],
            dst_ref=sums_in.at[way, dest],
            send_sem=sum_send_sem.at[way, dest],
            recv_sem=sum_recv_sem.at[way, dest],
            device_id={"chan": to},
            device_id_type=MESH,
        )

    last = chan_size - 1

    def pass_on(way, dest, to, has_earlier):
        project(dest)

        @pl.when(has_earlier)
        def _():
            sum_copy(way, dest, to).wait_recv()
            sums_out[way, dest] = (part[...] + sums_in[way, dest].astype(jnp.float32)).astype(
                jnp.bfloat16
            )

        @pl.when(jnp.logical_not(has_earlier))
        def _():
            sums_out[way, dest] = part[...].astype(jnp.bfloat16)

        sum_copy(way, dest, to).start()

    def sum_step(t, carry):
        up = last - (t - shard)

        @pl.when((t >= shard) & (up > shard))
        def _():
            pass_on(0, up, shard + 1, shard > 0)

        down = t - (last - shard)

        @pl.when((down >= 0) & (down < shard))
        def _():
            pass_on(1, down, shard - 1, shard < last)

        return carry

    lax.fori_loop(0, 2 * last, sum_step, 0)

    project(shard)
    part[...] += stream_ref[...].astype(jnp.float32)

    @pl.when(shard > 0)
    def _():
        sum_copy(0, shard, 0).wait_recv()
        part[...] += sums_in[0, shard].astype(jnp.float32)

    @pl.when(shard < last)
    def _():
        sum_copy(1, shard, 0).wait_recv()
        part[...] += sums_in[1, shard].astype(jnp.float32)

    out_ref[...] = part[...].astype(jnp.bfloat16)

    def drain(dest, carry):
        @pl.when(dest > shard)
        def _():
            sum_copy(0, dest, 0).wait_send()

        @pl.when(dest < shard)
        def _():
            sum_copy(1, dest, 0).wait_send()

        return carry

    lax.fori_loop(0, chan_size, drain, 0)


def mix(seq_size, chan_size, proj, stream, short_filter, decay_rate, residue, skip_gain, out_weight):
    rows, channels = stream.shape
    modes = decay_rate.shape[0]
    groups = channels // LANES
    f32, bf16 = jnp.float32, jnp.bfloat16
    vmem = pl.BlockSpec(memory_space=pltpu.VMEM)
    dma = pltpu.SemaphoreType.DMA
    return pl.pallas_call(
        functools.partial(block_kernel, seq_size, chan_size),
        out_shape=jax.ShapeDtypeStruct((rows, channels), bf16),
        in_specs=[vmem] * 6 + [pl.BlockSpec(memory_space=pl.ANY)],
        out_specs=vmem,
        scratch_shapes=[
            pltpu.VMEM((chan_size, channels, channels), bf16),
            pltpu.VMEM((FEAT, 8, channels), f32),
            pltpu.VMEM((FEAT, 8, channels), f32),
            pltpu.VMEM((FEAT, rows + 8, LANES), f32),
            pltpu.VMEM((groups, rows, LANES), f32),
            pltpu.VMEM((groups, rows, LANES), f32),
            pltpu.VMEM((groups, modes, SEGS, LANES), f32),
            pltpu.VMEM((modes, channels), f32),
            pltpu.VMEM((seq_size, modes, channels), f32),
            pltpu.VMEM((modes, channels), f32),
            pltpu.VMEM((modes, SEGS, LANES), f32),
            pltpu.VMEM((rows, LANES), f32),
            pltpu.VMEM((rows, channels), bf16),
            pltpu.VMEM((rows, channels), f32),
            pltpu.VMEM((2, chan_size, rows, channels), bf16),
            pltpu.VMEM((2, chan_size, rows, channels), bf16),
            dma((chan_size,)),
            dma((2,)),
            dma((seq_size,)),
            dma((seq_size,)),
            dma((2, chan_size)),
            dma((2, chan_size)),
        ],
        compiler_params=pltpu.CompilerParams(
            collective_id=0, has_side_effects=True, vmem_limit_bytes=48 << 20
        ),
    )(
        proj,
        stream,
        short_filter.reshape(FEAT * FEAT, channels),
        decay_rate,
        residue,
        skip_gain.reshape(1, channels),
        out_weight,
    )


def on_device(
    seq_size,
    chan_size,
    tokens,
    embedding,
    norm_gain,
    in_weight,
    short_filter,
    decay_rate,
    residue,
    skip_gain,
    out_weight,
):
    vocab_size = embedding.shape[0]
    one_hot = (tokens[:, None] == jnp.arange(vocab_size, dtype=jnp.int32)[None, :]).astype(
        jnp.bfloat16
    )
    stream = jnp.dot(one_hot, embedding, preferred_element_type=jnp.float32).astype(jnp.bfloat16)
    gathered = lax.all_gather(stream, "chan", axis=1, tiled=True)
    gathered_f = gathered.astype(jnp.float32)
    scale = lax.rsqrt(jnp.mean(gathered_f * gathered_f, axis=1, keepdims=True) + 1e-06)
    normed = (gathered_f * scale * norm_gain[None, :]).astype(jnp.bfloat16)
    proj = jnp.einsum("td,djc->jtc", normed, in_weight, preferred_element_type=jnp.float32).astype(
        jnp.bfloat16
    )
    return mix(
        seq_size, chan_size, proj, stream, short_filter, decay_rate, residue, skip_gain, out_weight
    )


def solution(mesh):
    placed = (
        P("seq"),
        P(None, "chan"),
        P(),
        P(None, None, "chan"),
        P(None, None, "chan"),
        P(None, "chan"),
        P(None, "chan"),
        P("chan"),
        P("chan", None),
    )
    return jax.shard_map(
        functools.partial(on_device, mesh.shape["seq"], mesh.shape["chan"]),
        mesh=mesh,
        in_specs=placed,
        out_specs=P("seq", "chan"),
        check_vma=False,
    )
```

```python
import functools

import jax
import jax.numpy as jnp
from jax import lax
from jax.experimental import pallas as pl
from jax.experimental.pallas import tpu as pltpu
from jax.sharding import PartitionSpec as P

FEAT = 3
LANES = 128
SEGS = 8
MESH = pl.DeviceIdType.MESH


def block_kernel(
    seq_size,
    chan_size,
    tokens_ref,
    embed_ref,
    norm_ref,
    filter_ref,
    decay_ref,
    residue_ref,
    skip_ref,
    in_weight_ref,
    weight_ref,
    out_ref,
    in_buf,
    weight_buf,
    gathered,
    squares_out,
    squares_in,
    normed,
    proj,
    rim_out,
    rim_in,
    padded,
    query_buf,
    driven_buf,
    seg_ends,
    own_end,
    all_ends,
    incoming,
    seg_starts,
    hidden_f,
    hidden,
    part,
    sums_out,
    sums_in,
    in_sem,
    weight_sem,
    square_send_sem,
    square_recv_sem,
    gather_send_sem,
    gather_recv_sem,
    rim_sem,
    end_send_sem,
    end_recv_sem,
    sum_send_sem,
    sum_recv_sem,
):
    place = lax.axis_index("seq")
    shard = lax.axis_index("chan")
    last = chan_size - 1
    rows = tokens_ref.shape[1]
    vocab, channels = embed_ref.shape
    modes = decay_ref.shape[0]
    groups = channels // LANES
    seg = rows // SEGS
    tile = min(256, channels)
    tiles = channels // tile

    def in_copy(d, j):
        depth = pl.ds(pl.multiple_of(d * channels, channels), channels)
        return pltpu.make_async_copy(
            in_weight_ref.at[j, depth, :], in_buf.at[d, j], in_sem.at[d, j]
        )

    def start_in(d):
        for j in range(FEAT):
            in_copy(d, j).start()

    start_in(shard)
    for k in range(1, chan_size):
        pl.when(shard - k >= 0)(functools.partial(start_in, shard - k))
        pl.when(shard + k <= last)(functools.partial(start_in, shard + k))
    weight_copies = [
        pltpu.make_async_copy(
            weight_ref.at[:, pl.ds(d * channels, channels)], weight_buf.at[d], weight_sem.at[d]
        )
        for d in range(chan_size)
    ]
    for copy in weight_copies:
        copy.start()

    barrier = pltpu.get_barrier_semaphore()
    for k in range(1, seq_size):
        pl.semaphore_signal(
            barrier, 1, device_id={"seq": lax.rem(place + k, seq_size)}, device_id_type=MESH
        )
    for k in range(1, chan_size):
        pl.semaphore_signal(
            barrier, 1, device_id={"chan": lax.rem(shard + k, chan_size)}, device_id_type=MESH
        )
    ids = lax.broadcasted_iota(jnp.int32, (vocab, rows), 0)
    one_hot = (ids == tokens_ref[...]).astype(jnp.float32).astype(jnp.bfloat16)
    stream = lax.dot_general(
        one_hot, embed_ref[...], (((0,), (0,)), ((), ())), preferred_element_type=jnp.float32
    )
    gathered[shard] = stream.astype(jnp.bfloat16)
    ones = jnp.ones((8, channels), jnp.float32)
    squares_out[...] = lax.dot_general(
        ones,
        stream * stream,
        (((1,), (1,)), ((), ())),
        precision=lax.Precision.HIGHEST,
        preferred_element_type=jnp.float32,
    )
    pl.semaphore_wait(barrier, seq_size - 1 + chan_size - 1)

    def square_copy(to, source):
        return pltpu.make_async_remote_copy(
            src_ref=squares_out,
            dst_ref=squares_in.at[source],
            send_sem=square_send_sem.at[to],
            recv_sem=square_recv_sem.at[source],
            device_id={"chan": to},
            device_id_type=MESH,
        )

    def gather_copy(way, which, to):
        return pltpu.make_async_remote_copy(
            src_ref=gathered.at[which],
            dst_ref=gathered.at[which],
            send_sem=gather_send_sem.at[way, which],
            recv_sem=gather_recv_sem.at[which],
            device_id={"chan": to},
            device_id_type=MESH,
        )

    for k in range(1, chan_size):
        square_copy(lax.rem(shard + k, chan_size), shard).start()

    def send_up(which):
        @pl.when(shard < last)
        def _():
            gather_copy(0, which, shard + 1).start()

    def send_down(which):
        @pl.when(shard > 0)
        def _():
            gather_copy(1, which, shard - 1).start()

    send_up(shard)
    send_down(shard)
    proj[...] = jnp.zeros_like(proj)
    total = squares_out[...]
    for k in range(1, chan_size):
        peer = lax.rem(shard + k, chan_size)
        square_copy(peer, shard).wait_send()
        square_copy(peer, peer).wait_recv()
        total = total + squares_in[peer]
    scale = lax.rsqrt(total.T[:, :1] * (1.0 / (channels * chan_size)) + 1e-06)

    def absorb(which):
        for j in range(FEAT):
            in_copy(which, j).wait()
        cols = pl.ds(pl.multiple_of(which * channels, channels), channels)
        normed[...] = (gathered[which].astype(jnp.float32) * scale * norm_ref[:, cols]).astype(
            jnp.bfloat16
        )

        def one(t, carry):
            j = t // tiles
            at = pl.ds(pl.multiple_of((t % tiles) * tile, tile), tile)
            proj[j, :, at] += jnp.dot(
                normed[...], in_buf[which, j, :, at], preferred_element_type=jnp.float32
            )
            return carry

        lax.fori_loop(0, FEAT * tiles, one, 0)

    absorb(shard)

    def gather_step(k, carry):
        below, above = shard - k, shard + k

        @pl.when(below >= 0)
        def _():
            gather_copy(0, below, 0).wait_recv()
            send_up(below)

        @pl.when(above <= last)
        def _():
            gather_copy(1, above, 0).wait_recv()
            send_down(above)

        pl.when(below >= 0)(functools.partial(absorb, below))
        pl.when(above <= last)(functools.partial(absorb, above))
        return carry

    lax.fori_loop(1, chan_size, gather_step, 0)

    def rounded(value):
        return value.astype(jnp.bfloat16).astype(jnp.float32)

    for j in range(FEAT):
        rim_out[j] = rounded(proj[j, rows - 8 :, :])
    rim_copy = pltpu.make_async_remote_copy(
        src_ref=rim_out,
        dst_ref=rim_in,
        send_sem=rim_sem.at[0],
        recv_sem=rim_sem.at[1],
        device_id={"seq": lax.rem(place + 1, seq_size)},
        device_id_type=MESH,
    )
    rim_copy.start()
    rim_copy.wait()
    keep = (place > 0).astype(jnp.float32)

    def spread(value):
        return jnp.broadcast_to(value[:, None, :], (value.shape[0], SEGS, LANES))

    def first_pass(g, carry):
        lanes = pl.ds(pl.multiple_of(g * LANES, LANES), LANES)
        feat = []
        for j in range(FEAT):
            now = rounded(proj[j, :, lanes])
            padded[j, 8:, :] = now
            padded[j, :8, :] = rim_in[j, :, lanes] * keep
            total = filter_ref[0, j : j + 1, lanes] * now
            for offset in range(1, FEAT):
                total = (
                    total
                    + filter_ref[offset, j : j + 1, lanes] * padded[j, pl.ds(8 - offset, rows), :]
                )
            feat.append(rounded(total))
        query_buf[g] = feat[0]
        driven_buf[g] = feat[1] * feat[2]
        decay = decay_ref[:, lanes]
        lam = spread(jnp.exp(-decay))

        def step(i, state):
            x = driven_buf[g, pl.ds(i, SEGS, stride=seg), :]
            return lam * state + x[None]

        state = lax.fori_loop(
            0, seg, step, jnp.zeros((modes, SEGS, LANES), jnp.float32), unroll=8
        )
        seg_ends[g] = state
        lam_seg = jnp.exp(-decay * seg)
        end = state[:, 0, :]
        for s in range(1, SEGS):
            end = lam_seg * end + state[:, s, :]
        own_end[:, lanes] = end
        return carry

    halves = 2 if groups > 1 else 1
    width = channels // halves
    per_half = groups // halves

    def end_copy(half, to, source):
        cols = pl.ds(half * width, width)
        return pltpu.make_async_remote_copy(
            src_ref=own_end.at[:, cols],
            dst_ref=all_ends.at[source, :, cols],
            send_sem=end_send_sem.at[half, to],
            recv_sem=end_recv_sem.at[half, source],
            device_id={"seq": to},
            device_id_type=MESH,
        )

    for half in range(halves):
        lax.fori_loop(half * per_half, (half + 1) * per_half, first_pass, 0)
        for k in range(1, seq_size):
            end_copy(half, lax.rem(place + k, seq_size), place).start()
    all_ends[place] = own_end[...]

    def second_pass(g, carry):
        lanes = pl.ds(pl.multiple_of(g * LANES, LANES), LANES)
        decay = decay_ref[:, lanes]
        lam_seg = jnp.exp(-decay * seg)
        start = incoming[:, lanes]
        for s in range(SEGS):
            seg_starts[:, s, :] = start
            start = lam_seg * start + seg_ends[g, :, s, :]
        lam = spread(jnp.exp(-decay))
        gain = spread(residue_ref[:, lanes])
        skip = jnp.broadcast_to(skip_ref[:, lanes], (SEGS, LANES))

        def step(i, state):
            at = pl.ds(i, SEGS, stride=seg)
            x = driven_buf[g, at, :]
            state = lam * state + x[None]
            long = jnp.sum(gain * state, axis=0) + skip * x
            hidden_f[at, :] = query_buf[g, at, :] * long
            return state

        lax.fori_loop(0, seg, step, seg_starts[...], unroll=8)
        hidden[:, lanes] = hidden_f[...].astype(jnp.bfloat16)
        return carry

    for half in range(halves):
        for k in range(1, seq_size):
            peer = lax.rem(place + k, seq_size)
            end_copy(half, peer, place).wait_send()
            end_copy(half, peer, peer).wait_recv()
        cols = slice(half * width, (half + 1) * width)
        span = jnp.exp(-decay_ref[:, cols] * rows)
        state = jnp.zeros((modes, width), jnp.float32)
        for p in range(seq_size - 1):
            state = jnp.where(p < place, span * state + all_ends[p, :, cols], state)
        incoming[:, cols] = state
        lax.fori_loop(half * per_half, (half + 1) * per_half, second_pass, 0)
    for copy in weight_copies:
        copy.wait()

    def project(dest):
        def one(t, carry):
            cols = pl.ds(pl.multiple_of(t * tile, tile), tile)
            part[:, cols] = jnp.dot(
                hidden[...], weight_buf[dest, :, cols], preferred_element_type=jnp.float32
            )
            return carry

        lax.fori_loop(0, tiles, one, 0)

    def sum_copy(way, dest, to):
        return pltpu.make_async_remote_copy(
            src_ref=sums_out.at[way, dest],
            dst_ref=sums_in.at[way, dest],
            send_sem=sum_send_sem.at[way, dest],
            recv_sem=sum_recv_sem.at[way, dest],
            device_id={"chan": to},
            device_id_type=MESH,
        )

    def pass_on(way, dest, to, has_earlier):
        project(dest)

        @pl.when(has_earlier)
        def _():
            sum_copy(way, dest, to).wait_recv()
            sums_out[way, dest] = (part[...] + sums_in[way, dest].astype(jnp.float32)).astype(
                jnp.bfloat16
            )

        @pl.when(jnp.logical_not(has_earlier))
        def _():
            sums_out[way, dest] = part[...].astype(jnp.bfloat16)

        sum_copy(way, dest, to).start()

    def sum_step(t, carry):
        up = last - (t - shard)

        @pl.when((t >= shard) & (up > shard))
        def _():
            pass_on(0, up, shard + 1, shard > 0)

        down = t - (last - shard)

        @pl.when((down >= 0) & (down < shard))
        def _():
            pass_on(1, down, shard - 1, shard < last)

        return carry

    lax.fori_loop(0, 2 * last, sum_step, 0)

    project(shard)
    part[...] += gathered[shard].astype(jnp.float32)

    @pl.when(shard > 0)
    def _():
        sum_copy(0, shard, 0).wait_recv()
        part[...] += sums_in[0, shard].astype(jnp.float32)

    @pl.when(shard < last)
    def _():
        sum_copy(1, shard, 0).wait_recv()
        part[...] += sums_in[1, shard].astype(jnp.float32)

    out_ref[...] = part[...].astype(jnp.bfloat16)

    def drain(dest, carry):
        @pl.when(dest > shard)
        def _():
            sum_copy(0, dest, 0).wait_send()

        @pl.when(dest < shard)
        def _():
            sum_copy(1, dest, 0).wait_send()

        @pl.when((dest <= shard) & (shard < last))
        def _():
            gather_copy(0, dest, 0).wait_send()

        @pl.when((dest >= shard) & (shard > 0))
        def _():
            gather_copy(1, dest, 0).wait_send()

        return carry

    lax.fori_loop(0, chan_size, drain, 0)


def on_device(
    seq_size,
    chan_size,
    tokens,
    embedding,
    norm_gain,
    in_weight,
    short_filter,
    decay_rate,
    residue,
    skip_gain,
    out_weight,
):
    rows = tokens.shape[0]
    channels = embedding.shape[1]
    modes = decay_rate.shape[0]
    groups = channels // LANES
    f32, bf16 = jnp.float32, jnp.bfloat16
    vmem = pl.BlockSpec(memory_space=pltpu.VMEM)
    hbm = pl.BlockSpec(memory_space=pl.ANY)
    dma = pltpu.SemaphoreType.DMA
    return pl.pallas_call(
        functools.partial(block_kernel, seq_size, chan_size),
        out_shape=jax.ShapeDtypeStruct((rows, channels), bf16),
        in_specs=[vmem] * 7 + [hbm] * 2,
        out_specs=vmem,
        scratch_shapes=[
            pltpu.VMEM((chan_size, FEAT, channels, channels), bf16),
            pltpu.VMEM((chan_size, channels, channels), bf16),
            pltpu.VMEM((chan_size, rows, channels), bf16),
            pltpu.VMEM((8, rows), f32),
            pltpu.VMEM((chan_size, 8, rows), f32),
            pltpu.VMEM((rows, channels), bf16),
            pltpu.VMEM((FEAT, rows, channels), f32),
            pltpu.VMEM((FEAT, 8, channels), f32),
            pltpu.VMEM((FEAT, 8, channels), f32),
            pltpu.VMEM((FEAT, rows + 8, LANES), f32),
            pltpu.VMEM((groups, rows, LANES), f32),
            pltpu.VMEM((groups, rows, LANES), f32),
            pltpu.VMEM((groups, modes, SEGS, LANES), f32),
            pltpu.VMEM((modes, channels), f32),
            pltpu.VMEM((seq_size, modes, channels), f32),
            pltpu.VMEM((modes, channels), f32),
            pltpu.VMEM((modes, SEGS, LANES), f32),
            pltpu.VMEM((rows, LANES), f32),
            pltpu.VMEM((rows, channels), bf16),
            pltpu.VMEM((rows, channels), f32),
            pltpu.VMEM((2, chan_size, rows, channels), bf16),
            pltpu.VMEM((2, chan_size, rows, channels), bf16),
            dma((chan_size, FEAT)),
            dma((chan_size,)),
            dma((chan_size,)),
            dma((chan_size,)),
            dma((2, chan_size)),
            dma((chan_size,)),
            dma((2,)),
            dma((2, seq_size)),
            dma((2, seq_size)),
            dma((2, chan_size)),
            dma((2, chan_size)),
        ],
        compiler_params=pltpu.CompilerParams(
            collective_id=0, has_side_effects=True, vmem_limit_bytes=60 << 20
        ),
    )(
        tokens.reshape(1, rows),
        embedding,
        norm_gain.reshape(1, -1),
        short_filter,
        decay_rate,
        residue,
        skip_gain.reshape(1, channels),
        in_weight.transpose(1, 0, 2),
        out_weight,
    )


def solution(mesh):
    placed = (
        P("seq"),
        P(None, "chan"),
        P(),
        P(None, None, "chan"),
        P(None, None, "chan"),
        P(None, "chan"),
        P(None, "chan"),
        P("chan"),
        P("chan", None),
    )
    return jax.shard_map(
        functools.partial(on_device, mesh.shape["seq"], mesh.shape["chan"]),
        mesh=mesh,
        in_specs=placed,
        out_specs=P("seq", "chan"),
        check_vma=False,
    )
```

```python
import functools

import jax
import jax.numpy as jnp
from jax import lax
from jax.experimental import pallas as pl
from jax.experimental.pallas import tpu as pltpu
from jax.sharding import PartitionSpec as P

FEAT = 3
LANES = 128
SEGS = 8
MESH = pl.DeviceIdType.MESH


def block_kernel(
    seq_size,
    chan_size,
    tokens_ref,
    embed_ref,
    norm_ref,
    filter_ref,
    decay_ref,
    residue_ref,
    skip_ref,
    in_weight_ref,
    weight_ref,
    out_ref,
    in_buf,
    weight_buf,
    tokens_in,
    gathered,
    squares_out,
    squares_in,
    normed,
    proj,
    rim_out,
    rim_in,
    padded,
    query_buf,
    driven_buf,
    seg_ends,
    own_end,
    all_ends,
    incoming,
    seg_starts,
    hidden_f,
    hidden,
    part,
    sums_out,
    sums_in,
    result_out,
    result_in,
    in_sem,
    weight_sem,
    token_send_sem,
    token_recv_sem,
    square_send_sem,
    square_recv_sem,
    gather_send_sem,
    gather_recv_sem,
    rim_send_sem,
    rim_recv_sem,
    end_send_sem,
    end_recv_sem,
    sum_send_sem,
    sum_recv_sem,
    result_send_sem,
    result_recv_sem,
):
    place = lax.axis_index("seq")
    shard = lax.axis_index("chan")
    last = chan_size - 1
    rows = tokens_ref.shape[2]
    vocab, channels = embed_ref.shape
    modes = decay_ref.shape[0]
    groups = channels // LANES
    seg = rows // SEGS
    tile = min(256, channels)
    tiles = channels // tile
    inner = (shard > 0) & (shard < last)
    outer = jnp.logical_not(inner)

    def in_copy(d, j):
        depth = pl.ds(pl.multiple_of(d * channels, channels), channels)
        return pltpu.make_async_copy(
            in_weight_ref.at[j, depth, :], in_buf.at[d, j], in_sem.at[d, j]
        )

    def start_in(d):
        for j in range(FEAT):
            in_copy(d, j).start()

    barrier = pltpu.get_barrier_semaphore()
    for k in range(1, seq_size):
        pl.semaphore_signal(
            barrier, 1, device_id={"seq": lax.rem(place + k, seq_size)}, device_id_type=MESH
        )
    for k in range(1, chan_size):
        pl.semaphore_signal(
            barrier, 1, device_id={"chan": lax.rem(shard + k, chan_size)}, device_id_type=MESH
        )

    start_in(shard)
    for k in range(1, chan_size):
        pl.when(shard - k >= 0)(functools.partial(start_in, shard - k))
        pl.when(shard + k <= last)(functools.partial(start_in, shard + k))
    weight_copies = [
        pltpu.make_async_copy(
            weight_ref.at[:, pl.ds(d * channels, channels)], weight_buf.at[d], weight_sem.at[d]
        )
        for d in range(chan_size)
    ]
    for copy in weight_copies:
        copy.start()
    pl.semaphore_wait(barrier, seq_size - 1 + chan_size - 1)

    def token_copy(half, phase, to):
        return pltpu.make_async_remote_copy(
            src_ref=tokens_ref.at[half],
            dst_ref=tokens_in.at[phase],
            send_sem=token_send_sem.at[half],
            recv_sem=token_recv_sem.at[phase],
            device_id={"seq": to},
            device_id_type=MESH,
        )

    for half in range(2):
        block = 2 * place + half
        phase, to = block // seq_size, lax.rem(block, seq_size)

        @pl.when(to != place)
        def _():
            token_copy(half, phase, to).start()

        @pl.when(to == place)
        def _():
            tokens_in[phase] = tokens_ref[half]

    def square_copy(h, to, source):
        return pltpu.make_async_remote_copy(
            src_ref=squares_out.at[h],
            dst_ref=squares_in.at[h, source],
            send_sem=square_send_sem.at[h, to],
            recv_sem=square_recv_sem.at[h, source],
            device_id={"chan": to},
            device_id_type=MESH,
        )

    def gather_copy(h, way, which, to):
        return pltpu.make_async_remote_copy(
            src_ref=gathered.at[h, which],
            dst_ref=gathered.at[h, which],
            send_sem=gather_send_sem.at[h, way, which],
            recv_sem=gather_recv_sem.at[h, which],
            device_id={"chan": to},
            device_id_type=MESH,
        )

    def send_up(h, which):
        @pl.when(shard < last)
        def _():
            gather_copy(h, 0, which, shard + 1).start()

    def send_down(h, which):
        @pl.when(shard > 0)
        def _():
            gather_copy(h, 1, which, shard - 1).start()

    def send_own(h):
        send_up(h, shard)
        send_down(h, shard)

    def look_up(h):
        source = (h * seq_size + place) // 2

        @pl.when(source != place)
        def _():
            token_copy(0, h, 0).wait_recv()

        ids = lax.broadcasted_iota(jnp.int32, (vocab, rows), 0)
        one_hot = (ids == tokens_in[h]).astype(jnp.float32).astype(jnp.bfloat16)
        stream = lax.dot_general(
            one_hot, embed_ref[...], (((0,), (0,)), ((), ())), preferred_element_type=jnp.float32
        )
        gathered[h, shard] = stream.astype(jnp.bfloat16)
        return stream

    def send_squares(h, stream):
        squares_out[h] = lax.dot_general(
            jnp.ones((8, channels), jnp.float32),
            stream * stream,
            (((1,), (1,)), ((), ())),
            precision=lax.Precision.HIGHEST,
            preferred_element_type=jnp.float32,
        )
        for k in range(1, chan_size):
            square_copy(h, lax.rem(shard + k, chan_size), shard).start()

    first = look_up(0)
    send_own(0)
    send_squares(0, first)
    second = look_up(1)
    pl.when(outer)(functools.partial(send_own, 1))
    send_squares(1, second)

    def row_scale(h):
        total = squares_out[h]
        for k in range(1, chan_size):
            peer = lax.rem(shard + k, chan_size)
            square_copy(h, peer, shard).wait_send()
            square_copy(h, peer, peer).wait_recv()
            total = total + squares_in[h, peer]
        return lax.rsqrt(total.T[:, :1] * (1.0 / (channels * chan_size)) + 1e-06)

    def gather(h):
        proj[...] = jnp.zeros_like(proj)
        scale = row_scale(h)

        def absorb(which):
            if h == 0:
                for j in range(FEAT):
                    in_copy(which, j).wait()
            cols = pl.ds(pl.multiple_of(which * channels, channels), channels)
            normed[...] = (
                gathered[h, which].astype(jnp.float32) * scale * norm_ref[:, cols]
            ).astype(jnp.bfloat16)

            def one(t, carry):
                j = t // tiles
                at = pl.ds(pl.multiple_of((t % tiles) * tile, tile), tile)
                proj[j, :, at] += jnp.dot(
                    normed[...], in_buf[which, j, :, at], preferred_element_type=jnp.float32
                )
                return carry

            lax.fori_loop(0, FEAT * tiles, one, 0)

        if h == 0:
            absorb(shard)
        else:
            pl.when(outer)(functools.partial(absorb, shard))

        def gather_step(k, carry):
            below, above = shard - k, shard + k

            @pl.when(below >= 0)
            def _():
                gather_copy(h, 0, below, 0).wait_recv()
                send_up(h, below)

            @pl.when(above <= last)
            def _():
                gather_copy(h, 1, above, 0).wait_recv()
                send_down(h, above)

            pl.when(below >= 0)(functools.partial(absorb, below))
            pl.when(above <= last)(functools.partial(absorb, above))
            return carry

        lax.fori_loop(1, chan_size, gather_step, 0)
        if h == 1:
            pl.when(inner)(functools.partial(absorb, shard))

    def rounded(value):
        return value.astype(jnp.bfloat16).astype(jnp.float32)

    def spread(value):
        return jnp.broadcast_to(value[:, None, :], (value.shape[0], SEGS, LANES))

    halves = 2 if groups > 1 else 1
    width = channels // halves
    per_half = groups // halves

    def middle(h):
        for j in range(FEAT):
            rim_out[h, j] = rounded(proj[j, rows - 8 :, :])
        rim_copy = pltpu.make_async_remote_copy(
            src_ref=rim_out.at[h],
            dst_ref=rim_in.at[h],
            send_sem=rim_send_sem.at[h],
            recv_sem=rim_recv_sem.at[h],
            device_id={"seq": lax.rem(place + 1, seq_size)},
            device_id_type=MESH,
        )
        rim_copy.start()
        rim_copy.wait()

        def first_pass(g, carry):
            lanes = pl.ds(pl.multiple_of(g * LANES, LANES), LANES)
            feat = []
            for j in range(FEAT):
                now = rounded(proj[j, :, lanes])
                before = 0.0 if h == 0 else rim_in[0, j, :, lanes]
                padded[j, 8:, :] = now
                padded[j, :8, :] = jnp.where(place > 0, rim_in[h, j, :, lanes], before)
                total = filter_ref[0, j : j + 1, lanes] * now
                for offset in range(1, FEAT):
                    total = (
                        total
                        + filter_ref[offset, j : j + 1, lanes]
                        * padded[j, pl.ds(8 - offset, rows), :]
                    )
                feat.append(rounded(total))
            query_buf[g] = feat[0]
            driven_buf[g] = feat[1] * feat[2]
            decay = decay_ref[:, lanes]
            lam = spread(jnp.exp(-decay))

            def step(i, state):
                x = driven_buf[g, pl.ds(i, SEGS, stride=seg), :]
                return lam * state + x[None]

            state = lax.fori_loop(
                0, seg, step, jnp.zeros((modes, SEGS, LANES), jnp.float32), unroll=8
            )
            seg_ends[g] = state
            lam_seg = jnp.exp(-decay * seg)
            end = state[:, 0, :]
            for s in range(1, SEGS):
                end = lam_seg * end + state[:, s, :]
            own_end[:, lanes] = end
            return carry

        def end_copy(half, to, source):
            cols = pl.ds(half * width, width)
            return pltpu.make_async_remote_copy(
                src_ref=own_end.at[:, cols],
                dst_ref=all_ends.at[h, source, :, cols],
                send_sem=end_send_sem.at[h, half, to],
                recv_sem=end_recv_sem.at[h, half, source],
                device_id={"seq": to},
                device_id_type=MESH,
            )

        for half in range(halves):
            lax.fori_loop(half * per_half, (half + 1) * per_half, first_pass, 0)
            for k in range(1, seq_size):
                end_copy(half, lax.rem(place + k, seq_size), place).start()
        all_ends[h, place] = own_end[...]

        def second_pass(g, carry):
            lanes = pl.ds(pl.multiple_of(g * LANES, LANES), LANES)
            decay = decay_ref[:, lanes]
            lam_seg = jnp.exp(-decay * seg)
            start = incoming[:, lanes]
            for s in range(SEGS):
                seg_starts[:, s, :] = start
                start = lam_seg * start + seg_ends[g, :, s, :]
            lam = spread(jnp.exp(-decay))
            gain = spread(residue_ref[:, lanes])
            skip = jnp.broadcast_to(skip_ref[:, lanes], (SEGS, LANES))

            def step(i, state):
                at = pl.ds(i, SEGS, stride=seg)
                x = driven_buf[g, at, :]
                state = lam * state + x[None]
                long = jnp.sum(gain * state, axis=0) + skip * x
                hidden_f[at, :] = query_buf[g, at, :] * long
                return state

            lax.fori_loop(0, seg, step, seg_starts[...], unroll=8)
            hidden[h, :, lanes] = hidden_f[...].astype(jnp.bfloat16)
            return carry

        for half in range(halves):
            for k in range(1, seq_size):
                peer = lax.rem(place + k, seq_size)
                end_copy(half, peer, place).wait_send()
                end_copy(half, peer, peer).wait_recv()
            cols = slice(half * width, (half + 1) * width)
            span = jnp.exp(-decay_ref[:, cols] * rows)
            state = jnp.zeros((modes, width), jnp.float32)
            if h == 1:
                for p in range(seq_size):
                    state = span * state + all_ends[0, p, :, cols]
            for p in range(seq_size - 1):
                state = jnp.where(p < place, span * state + all_ends[h, p, :, cols], state)
            incoming[:, cols] = state
            lax.fori_loop(half * per_half, (half + 1) * per_half, second_pass, 0)

    def project(h, dest):
        def one(t, carry):
            cols = pl.ds(pl.multiple_of(t * tile, tile), tile)
            part[:, cols] = jnp.dot(
                hidden[h], weight_buf[dest, :, cols], preferred_element_type=jnp.float32
            )
            return carry

        lax.fori_loop(0, tiles, one, 0)

    def sum_copy(h, way, dest, to):
        return pltpu.make_async_remote_copy(
            src_ref=sums_out.at[h, way, dest],
            dst_ref=sums_in.at[h, way, dest],
            send_sem=sum_send_sem.at[h, way, dest],
            recv_sem=sum_recv_sem.at[h, way, dest],
            device_id={"chan": to},
            device_id_type=MESH,
        )

    def begin_sums(h):
        def begin(way, dest, to):
            project(h, dest)
            sums_out[h, way, dest] = part[...].astype(jnp.bfloat16)
            sum_copy(h, way, dest, to).start()

        def one(i, carry):
            pl.when(shard == 0)(functools.partial(begin, 0, last - i, shard + 1))
            pl.when(shard == last)(functools.partial(begin, 1, i, shard - 1))
            return carry

        lax.fori_loop(0, last, one, 0)

    def add_sums(h):
        def pass_on(way, dest, to):
            project(h, dest)
            sum_copy(h, way, dest, to).wait_recv()
            sums_out[h, way, dest] = (
                part[...] + sums_in[h, way, dest].astype(jnp.float32)
            ).astype(jnp.bfloat16)
            sum_copy(h, way, dest, to).start()

        def sum_step(t, carry):
            up = last - (t - shard)
            pl.when(inner & (t >= shard) & (up > shard))(
                functools.partial(pass_on, 0, up, shard + 1)
            )
            down = t - (last - shard)
            pl.when(inner & (down >= 0) & (down < shard))(
                functools.partial(pass_on, 1, down, shard - 1)
            )
            return carry

        lax.fori_loop(0, 2 * last, sum_step, 0)

    def result_copy(h, half, to):
        return pltpu.make_async_remote_copy(
            src_ref=result_out.at[h],
            dst_ref=result_in.at[half],
            send_sem=result_send_sem.at[h],
            recv_sem=result_recv_sem.at[half],
            device_id={"seq": to},
            device_id_type=MESH,
        )

    def finish(h):
        project(h, shard)
        part[...] += gathered[h, shard].astype(jnp.float32)

        @pl.when(shard > 0)
        def _():
            sum_copy(h, 0, shard, 0).wait_recv()
            part[...] += sums_in[h, 0, shard].astype(jnp.float32)

        @pl.when(shard < last)
        def _():
            sum_copy(h, 1, shard, 0).wait_recv()
            part[...] += sums_in[h, 1, shard].astype(jnp.float32)

        block = h * seq_size + place
        to, half = block // 2, lax.rem(block, 2)
        result_out[h] = part[...].astype(jnp.bfloat16)

        @pl.when(to != place)
        def _():
            result_copy(h, half, to).start()

        @pl.when(to == place)
        def _():
            result_in[half] = result_out[h]

    gather(0)
    pl.when(inner)(functools.partial(send_own, 1))
    middle(0)
    for copy in weight_copies:
        copy.wait()
    begin_sums(0)
    gather(1)
    middle(1)
    begin_sums(1)
    add_sums(0)
    finish(0)
    add_sums(1)
    finish(1)

    for h in range(2):
        block = h * seq_size + place

        @pl.when(block // 2 != place)
        def _():
            result_copy(h, 0, 0).wait_send()

        def drain(dest, carry):
            @pl.when(dest > shard)
            def _():
                sum_copy(h, 0, dest, 0).wait_send()

            @pl.when(dest < shard)
            def _():
                sum_copy(h, 1, dest, 0).wait_send()

            @pl.when((dest <= shard) & (shard < last))
            def _():
                gather_copy(h, 0, dest, 0).wait_send()

            @pl.when((dest >= shard) & (shard > 0))
            def _():
                gather_copy(h, 1, dest, 0).wait_send()

            return carry

        lax.fori_loop(0, chan_size, drain, 0)

    for half in range(2):
        block = 2 * place + half

        @pl.when(lax.rem(block, seq_size) != place)
        def _():
            token_copy(half, 0, 0).wait_send()
            result_copy(0, half, 0).wait_recv()

        out_ref[half * rows : (half + 1) * rows, :] = result_in[half]


def on_device(
    seq_size,
    chan_size,
    tokens,
    embedding,
    norm_gain,
    in_weight,
    short_filter,
    decay_rate,
    residue,
    skip_gain,
    out_weight,
):
    rows = tokens.shape[0] // 2
    channels = embedding.shape[1]
    modes = decay_rate.shape[0]
    groups = channels // LANES
    f32, bf16 = jnp.float32, jnp.bfloat16
    vmem = pl.BlockSpec(memory_space=pltpu.VMEM)
    hbm = pl.BlockSpec(memory_space=pl.ANY)
    dma = pltpu.SemaphoreType.DMA
    return pl.pallas_call(
        functools.partial(block_kernel, seq_size, chan_size),
        out_shape=jax.ShapeDtypeStruct((2 * rows, channels), bf16),
        in_specs=[vmem] * 7 + [hbm] * 2,
        out_specs=vmem,
        scratch_shapes=[
            pltpu.VMEM((chan_size, FEAT, channels, channels), bf16),
            pltpu.VMEM((chan_size, channels, channels), bf16),
            pltpu.VMEM((2, 1, rows), jnp.int32),
            pltpu.VMEM((2, chan_size, rows, channels), bf16),
            pltpu.VMEM((2, 8, rows), f32),
            pltpu.VMEM((2, chan_size, 8, rows), f32),
            pltpu.VMEM((rows, channels), bf16),
            pltpu.VMEM((FEAT, rows, channels), f32),
            pltpu.VMEM((2, FEAT, 8, channels), f32),
            pltpu.VMEM((2, FEAT, 8, channels), f32),
            pltpu.VMEM((FEAT, rows + 8, LANES), f32),
            pltpu.VMEM((groups, rows, LANES), f32),
            pltpu.VMEM((groups, rows, LANES), f32),
            pltpu.VMEM((groups, modes, SEGS, LANES), f32),
            pltpu.VMEM((modes, channels), f32),
            pltpu.VMEM((2, seq_size, modes, channels), f32),
            pltpu.VMEM((modes, channels), f32),
            pltpu.VMEM((modes, SEGS, LANES), f32),
            pltpu.VMEM((rows, LANES), f32),
            pltpu.VMEM((2, rows, channels), bf16),
            pltpu.VMEM((rows, channels), f32),
            pltpu.VMEM((2, 2, chan_size, rows, channels), bf16),
            pltpu.VMEM((2, 2, chan_size, rows, channels), bf16),
            pltpu.VMEM((2, rows, channels), bf16),
            pltpu.VMEM((2, rows, channels), bf16),
            dma((chan_size, FEAT)),
            dma((chan_size,)),
            dma((2,)),
            dma((2,)),
            dma((2, chan_size)),
            dma((2, chan_size)),
            dma((2, 2, chan_size)),
            dma((2, chan_size)),
            dma((2,)),
            dma((2,)),
            dma((2, 2, seq_size)),
            dma((2, 2, seq_size)),
            dma((2, 2, chan_size)),
            dma((2, 2, chan_size)),
            dma((2,)),
            dma((2,)),
        ],
        compiler_params=pltpu.CompilerParams(
            collective_id=0, has_side_effects=True, vmem_limit_bytes=60 << 20
        ),
    )(
        tokens.reshape(2, 1, rows),
        embedding,
        norm_gain.reshape(1, -1),
        short_filter,
        decay_rate,
        residue,
        skip_gain.reshape(1, channels),
        in_weight.transpose(1, 0, 2),
        out_weight,
    )


def solution(mesh):
    placed = (
        P("seq"),
        P(None, "chan"),
        P(),
        P(None, None, "chan"),
        P(None, None, "chan"),
        P(None, "chan"),
        P(None, "chan"),
        P("chan"),
        P("chan", None),
    )
    return jax.shard_map(
        functools.partial(on_device, mesh.shape["seq"], mesh.shape["chan"]),
        mesh=mesh,
        in_specs=placed,
        out_specs=P("seq", "chan"),
        check_vma=False,
    )
```

```python
import functools

import jax
import jax.numpy as jnp
from jax import lax
from jax.experimental import pallas as pl
from jax.experimental.pallas import tpu as pltpu
from jax.sharding import PartitionSpec as P

FEAT = 3
LANES = 128
SEGS = 8
MESH = pl.DeviceIdType.MESH


def block_kernel(
    seq_size,
    chan_size,
    tokens_ref,
    embed_ref,
    norm_ref,
    filter_ref,
    decay_ref,
    residue_ref,
    skip_ref,
    in_weight_ref,
    weight_ref,
    out_ref,
    in_buf,
    weight_buf,
    tokens_in,
    gathered,
    squares_out,
    squares_in,
    normed,
    proj,
    rim_out,
    rim_in,
    padded,
    query_buf,
    driven_buf,
    seg_ends,
    own_end,
    all_ends,
    incoming,
    factors,
    hidden_f,
    hidden,
    part,
    sums_out,
    sums_in,
    result_out,
    result_in,
    in_sem,
    weight_sem,
    token_send_sem,
    token_recv_sem,
    square_send_sem,
    square_recv_sem,
    gather_send_sem,
    gather_recv_sem,
    rim_send_sem,
    rim_recv_sem,
    end_send_sem,
    end_recv_sem,
    sum_send_sem,
    sum_recv_sem,
    result_send_sem,
    result_recv_sem,
):
    place = lax.axis_index("seq")
    shard = lax.axis_index("chan")
    last = chan_size - 1
    rows = tokens_ref.shape[2]
    vocab, channels = embed_ref.shape
    modes = decay_ref.shape[0]
    groups = channels // LANES
    seg = rows // SEGS
    tile = min(256, channels)
    tiles = channels // tile
    inner = (shard > 0) & (shard < last)
    outer = jnp.logical_not(inner)

    def in_copy(d, j):
        depth = pl.ds(pl.multiple_of(d * channels, channels), channels)
        return pltpu.make_async_copy(
            in_weight_ref.at[j, depth, :], in_buf.at[d, j], in_sem.at[d, j]
        )

    def start_in(d):
        for j in range(FEAT):
            in_copy(d, j).start()

    barrier = pltpu.get_barrier_semaphore()
    for k in range(1, seq_size):
        pl.semaphore_signal(
            barrier, 1, device_id={"seq": lax.rem(place + k, seq_size)}, device_id_type=MESH
        )
    for k in range(1, chan_size):
        pl.semaphore_signal(
            barrier, 1, device_id={"chan": lax.rem(shard + k, chan_size)}, device_id_type=MESH
        )

    start_in(shard)
    for k in range(1, chan_size):
        pl.when(shard - k >= 0)(functools.partial(start_in, shard - k))
        pl.when(shard + k <= last)(functools.partial(start_in, shard + k))
    weight_copies = [
        pltpu.make_async_copy(
            weight_ref.at[:, pl.ds(d * channels, channels)], weight_buf.at[d], weight_sem.at[d]
        )
        for d in range(chan_size)
    ]
    for copy in weight_copies:
        copy.start()
    pl.semaphore_wait(barrier, seq_size - 1 + chan_size - 1)

    def token_copy(half, phase, to):
        return pltpu.make_async_remote_copy(
            src_ref=tokens_ref.at[half],
            dst_ref=tokens_in.at[phase],
            send_sem=token_send_sem.at[half],
            recv_sem=token_recv_sem.at[phase],
            device_id={"seq": to},
            device_id_type=MESH,
        )

    for half in range(2):
        block = 2 * place + half
        phase, to = block // seq_size, lax.rem(block, seq_size)

        @pl.when(to != place)
        def _():
            token_copy(half, phase, to).start()

        @pl.when(to == place)
        def _():
            tokens_in[phase] = tokens_ref[half]

    def square_copy(h, to, source):
        return pltpu.make_async_remote_copy(
            src_ref=squares_out.at[h],
            dst_ref=squares_in.at[h, source],
            send_sem=square_send_sem.at[h, to],
            recv_sem=square_recv_sem.at[h, source],
            device_id={"chan": to},
            device_id_type=MESH,
        )

    def gather_copy(h, way, which, to):
        return pltpu.make_async_remote_copy(
            src_ref=gathered.at[h, which],
            dst_ref=gathered.at[h, which],
            send_sem=gather_send_sem.at[h, way, which],
            recv_sem=gather_recv_sem.at[h, which],
            device_id={"chan": to},
            device_id_type=MESH,
        )

    def send_up(h, which):
        @pl.when(shard < last)
        def _():
            gather_copy(h, 0, which, shard + 1).start()

    def send_down(h, which):
        @pl.when(shard > 0)
        def _():
            gather_copy(h, 1, which, shard - 1).start()

    def send_own(h):
        send_up(h, shard)
        send_down(h, shard)

    def look_up(h):
        source = (h * seq_size + place) // 2

        @pl.when(source != place)
        def _():
            token_copy(0, h, 0).wait_recv()

        ids = lax.broadcasted_iota(jnp.int32, (vocab, rows), 0)
        one_hot = (ids == tokens_in[h]).astype(jnp.float32).astype(jnp.bfloat16)
        stream = lax.dot_general(
            one_hot, embed_ref[...], (((0,), (0,)), ((), ())), preferred_element_type=jnp.float32
        )
        gathered[h, shard] = stream.astype(jnp.bfloat16)
        return stream

    def send_squares(h, stream):
        squares_out[h] = lax.dot_general(
            jnp.ones((8, channels), jnp.float32),
            stream * stream,
            (((1,), (1,)), ((), ())),
            precision=lax.Precision.HIGHEST,
            preferred_element_type=jnp.float32,
        )
        for k in range(1, chan_size):
            square_copy(h, lax.rem(shard + k, chan_size), shard).start()

    first = look_up(0)
    send_own(0)
    second = look_up(1)
    pl.when(outer)(functools.partial(send_own, 1))
    send_squares(0, first)
    send_squares(1, second)

    def spread(value):
        return jnp.broadcast_to(value[:, None, :], (value.shape[0], SEGS, LANES))

    def make_factors(g, carry):
        lanes = pl.ds(pl.multiple_of(g * LANES, LANES), LANES)
        decay = spread(decay_ref[:, lanes])
        left = (SEGS - 1 - lax.broadcasted_iota(jnp.int32, (1, SEGS, LANES), 1)) * seg
        factors[0, g] = jnp.exp(-decay)
        factors[1, g] = spread(residue_ref[:, lanes])
        factors[2, g] = jnp.exp(-decay * seg)
        factors[3, g] = jnp.exp(-decay * left.astype(jnp.float32))
        return carry

    lax.fori_loop(0, groups, make_factors, 0)
    proj[...] = jnp.zeros_like(proj)

    def row_scale(h):
        total = squares_out[h]
        for k in range(1, chan_size):
            peer = lax.rem(shard + k, chan_size)
            square_copy(h, peer, shard).wait_send()
            square_copy(h, peer, peer).wait_recv()
            total = total + squares_in[h, peer]
        return lax.rsqrt(total.T[:, :1] * (1.0 / (channels * chan_size)) + 1e-06)

    scales = [row_scale(0), row_scale(1)]

    def absorb(h, which):
        cols = pl.ds(pl.multiple_of(which * channels, channels), channels)
        normed[...] = (
            gathered[h, which].astype(jnp.float32) * scales[h] * norm_ref[:, cols]
        ).astype(jnp.bfloat16)

        def one(t, carry):
            j = t // tiles
            at = pl.ds(pl.multiple_of((t % tiles) * tile, tile), tile)
            proj[h, j, :, at] += jnp.dot(
                normed[...], in_buf[which, j, :, at], preferred_element_type=jnp.float32
            )
            return carry

        lax.fori_loop(0, FEAT * tiles, one, 0)

    def gather(h):
        def take(which):
            if h == 0:
                for j in range(FEAT):
                    in_copy(which, j).wait()
            absorb(h, which)

        if h == 0:
            take(shard)
            absorb(1, shard)

        def gather_step(k, carry):
            below, above = shard - k, shard + k

            @pl.when(below >= 0)
            def _():
                gather_copy(h, 0, below, 0).wait_recv()
                send_up(h, below)

            @pl.when(above <= last)
            def _():
                gather_copy(h, 1, above, 0).wait_recv()
                send_down(h, above)

            pl.when(below >= 0)(functools.partial(take, below))
            pl.when(above <= last)(functools.partial(take, above))
            return carry

        lax.fori_loop(1, chan_size, gather_step, 0)

    def rounded(value):
        return value.astype(jnp.bfloat16).astype(jnp.float32)

    sublane = lax.broadcasted_iota(jnp.int32, (1, SEGS, LANES), 1)

    def shifted(value, by):
        return pltpu.roll(value, by, axis=1)

    halves = 2 if groups > 1 else 1
    width = channels // halves
    per_half = groups // halves

    def middle(h):
        for j in range(FEAT):
            rim_out[h, j] = rounded(proj[h, j, rows - 8 :, :])
        rim_copy = pltpu.make_async_remote_copy(
            src_ref=rim_out.at[h],
            dst_ref=rim_in.at[h],
            send_sem=rim_send_sem.at[h],
            recv_sem=rim_recv_sem.at[h],
            device_id={"seq": lax.rem(place + 1, seq_size)},
            device_id_type=MESH,
        )
        rim_copy.start()

        def featurize(g, count, with_rim):
            lanes = pl.ds(pl.multiple_of(g * LANES, LANES), LANES)
            feat = []
            for j in range(FEAT):
                now = rounded(proj[h, j, :count, lanes])
                padded[j, 8 : 8 + count, :] = now
                if with_rim:
                    before = 0.0 if h == 0 else rim_in[0, j, :, lanes]
                    padded[j, :8, :] = jnp.where(place > 0, rim_in[h, j, :, lanes], before)
                else:
                    padded[j, :8, :] = jnp.zeros((8, LANES), jnp.float32)
                total = filter_ref[0, j : j + 1, lanes] * now
                for offset in range(1, FEAT):
                    total = (
                        total
                        + filter_ref[offset, j : j + 1, lanes]
                        * padded[j, pl.ds(8 - offset, count), :]
                    )
                feat.append(rounded(total))
            query_buf[g, :count, :] = feat[0]
            driven_buf[g, :count, :] = feat[1] * feat[2]

        def feature_pass(g, carry):
            featurize(g, rows, False)
            return carry

        def first_pass(g, carry):
            lanes = pl.ds(pl.multiple_of(g * LANES, LANES), LANES)
            featurize(g, 16, True)
            lam = factors[0, g]

            def step(i, state):
                x = driven_buf[g, pl.ds(i, SEGS, stride=seg), :]
                return lam * state + x[None]

            state = lax.fori_loop(
                0, seg, step, jnp.zeros((modes, SEGS, LANES), jnp.float32), unroll=8
            )
            seg_ends[g] = state
            end = factors[3, g] * state
            for by in (4, 2, 1):
                end = end + shifted(end, by)
            end = end.reshape(modes // SEGS, SEGS, SEGS, LANES)
            mode = lax.broadcasted_iota(jnp.int32, (1, SEGS, SEGS, LANES), 1)
            row = lax.broadcasted_iota(jnp.int32, (1, SEGS, SEGS, LANES), 2)
            end = jnp.sum(jnp.where(mode == row, end, 0.0), axis=1)
            own_end[:, lanes] = end.reshape(modes, LANES)
            return carry

        def end_copy(half, to, source):
            cols = pl.ds(half * width, width)
            return pltpu.make_async_remote_copy(
                src_ref=own_end.at[:, cols],
                dst_ref=all_ends.at[h, source, :, cols],
                send_sem=end_send_sem.at[h, half, to],
                recv_sem=end_recv_sem.at[h, half, source],
                device_id={"seq": to},
                device_id_type=MESH,
            )

        for half in range(halves):
            lax.fori_loop(half * per_half, (half + 1) * per_half, feature_pass, 0)
            if half == 0:
                rim_copy.wait()
            lax.fori_loop(half * per_half, (half + 1) * per_half, first_pass, 0)
            for k in range(1, seq_size):
                end_copy(half, lax.rem(place + k, seq_size), place).start()
        all_ends[h, place] = own_end[...]

        def second_pass(g, carry):
            lanes = pl.ds(pl.multiple_of(g * LANES, LANES), LANES)
            start = jnp.where(sublane > 0, shifted(seg_ends[g], 1), spread(incoming[:, lanes]))
            power = factors[2, g]
            for by in (1, 2, 4):
                start = start + jnp.where(sublane >= by, power * shifted(start, by), 0.0)
                power = power * power
            lam = factors[0, g]
            gain = factors[1, g]
            skip = jnp.broadcast_to(skip_ref[:, lanes], (SEGS, LANES))

            def step(i, state):
                at = pl.ds(i, SEGS, stride=seg)
                x = driven_buf[g, at, :]
                state = lam * state + x[None]
                long = jnp.sum(gain * state, axis=0) + skip * x
                hidden_f[at, :] = query_buf[g, at, :] * long
                return state

            lax.fori_loop(0, seg, step, start, unroll=8)
            hidden[h, :, lanes] = hidden_f[...].astype(jnp.bfloat16)
            return carry

        for half in range(halves):
            for k in range(1, seq_size):
                peer = lax.rem(place + k, seq_size)
                end_copy(half, peer, place).wait_send()
                end_copy(half, peer, peer).wait_recv()
            cols = slice(half * width, (half + 1) * width)
            span = jnp.exp(-decay_ref[:, cols] * rows)
            state = jnp.zeros((modes, width), jnp.float32)
            if h == 1:
                for p in range(seq_size):
                    state = span * state + all_ends[0, p, :, cols]
            for p in range(seq_size - 1):
                state = jnp.where(p < place, span * state + all_ends[h, p, :, cols], state)
            incoming[:, cols] = state
            lax.fori_loop(half * per_half, (half + 1) * per_half, second_pass, 0)

    def project(h, dest):
        def one(t, carry):
            cols = pl.ds(pl.multiple_of(t * tile, tile), tile)
            part[:, cols] = jnp.dot(
                hidden[h], weight_buf[dest, :, cols], preferred_element_type=jnp.float32
            )
            return carry

        lax.fori_loop(0, tiles, one, 0)

    def sum_copy(h, way, dest, to):
        return pltpu.make_async_remote_copy(
            src_ref=sums_out.at[h, way, dest],
            dst_ref=sums_in.at[h, way, dest],
            send_sem=sum_send_sem.at[h, way, dest],
            recv_sem=sum_recv_sem.at[h, way, dest],
            device_id={"chan": to},
            device_id_type=MESH,
        )

    def begin_sums(h):
        def begin(way, dest, to):
            project(h, dest)
            sums_out[h, way, dest] = part[...].astype(jnp.bfloat16)
            sum_copy(h, way, dest, to).start()

        def one(i, carry):
            pl.when(shard == 0)(functools.partial(begin, 0, last - i, shard + 1))
            pl.when(shard == last)(functools.partial(begin, 1, i, shard - 1))
            return carry

        lax.fori_loop(0, last, one, 0)

    def add_sums(h):
        def pass_on(way, dest, to):
            project(h, dest)
            sum_copy(h, way, dest, to).wait_recv()
            sums_out[h, way, dest] = (
                part[...] + sums_in[h, way, dest].astype(jnp.float32)
            ).astype(jnp.bfloat16)
            sum_copy(h, way, dest, to).start()

        def sum_step(t, carry):
            up = last - (t - shard)
            pl.when(inner & (t >= shard) & (up > shard))(
                functools.partial(pass_on, 0, up, shard + 1)
            )
            down = t - (last - shard)
            pl.when(inner & (down >= 0) & (down < shard))(
                functools.partial(pass_on, 1, down, shard - 1)
            )
            return carry

        lax.fori_loop(0, 2 * last, sum_step, 0)

    def result_copy(h, half, to):
        return pltpu.make_async_remote_copy(
            src_ref=result_out.at[h],
            dst_ref=result_in.at[half],
            send_sem=result_send_sem.at[h],
            recv_sem=result_recv_sem.at[half],
            device_id={"seq": to},
            device_id_type=MESH,
        )

    def finish(h):
        project(h, shard)
        part[...] += gathered[h, shard].astype(jnp.float32)

        @pl.when(shard > 0)
        def _():
            sum_copy(h, 0, shard, 0).wait_recv()
            part[...] += sums_in[h, 0, shard].astype(jnp.float32)

        @pl.when(shard < last)
        def _():
            sum_copy(h, 1, shard, 0).wait_recv()
            part[...] += sums_in[h, 1, shard].astype(jnp.float32)

        block = h * seq_size + place
        to, half = block // 2, lax.rem(block, 2)
        result_out[h] = part[...].astype(jnp.bfloat16)

        @pl.when(to != place)
        def _():
            result_copy(h, half, to).start()

        @pl.when(to == place)
        def _():
            result_in[half] = result_out[h]

    gather(0)
    pl.when(inner)(functools.partial(send_own, 1))
    middle(0)
    for copy in weight_copies:
        copy.wait()
    begin_sums(0)
    gather(1)
    middle(1)
    begin_sums(1)
    add_sums(0)
    finish(0)
    add_sums(1)
    finish(1)

    for h in range(2):
        block = h * seq_size + place

        @pl.when(block // 2 != place)
        def _():
            result_copy(h, 0, 0).wait_send()

        def drain(dest, carry):
            @pl.when(dest > shard)
            def _():
                sum_copy(h, 0, dest, 0).wait_send()

            @pl.when(dest < shard)
            def _():
                sum_copy(h, 1, dest, 0).wait_send()

            @pl.when((dest <= shard) & (shard < last))
            def _():
                gather_copy(h, 0, dest, 0).wait_send()

            @pl.when((dest >= shard) & (shard > 0))
            def _():
                gather_copy(h, 1, dest, 0).wait_send()

            return carry

        lax.fori_loop(0, chan_size, drain, 0)

    for half in range(2):
        block = 2 * place + half

        @pl.when(lax.rem(block, seq_size) != place)
        def _():
            token_copy(half, 0, 0).wait_send()
            result_copy(0, half, 0).wait_recv()

        out_ref[half * rows : (half + 1) * rows, :] = result_in[half]


def on_device(
    seq_size,
    chan_size,
    tokens,
    embedding,
    norm_gain,
    in_weight,
    short_filter,
    decay_rate,
    residue,
    skip_gain,
    out_weight,
):
    rows = tokens.shape[0] // 2
    channels = embedding.shape[1]
    modes = decay_rate.shape[0]
    groups = channels // LANES
    f32, bf16 = jnp.float32, jnp.bfloat16
    vmem = pl.BlockSpec(memory_space=pltpu.VMEM)
    hbm = pl.BlockSpec(memory_space=pl.ANY)
    dma = pltpu.SemaphoreType.DMA
    return pl.pallas_call(
        functools.partial(block_kernel, seq_size, chan_size),
        out_shape=jax.ShapeDtypeStruct((2 * rows, channels), bf16),
        in_specs=[vmem] * 7 + [hbm] * 2,
        out_specs=vmem,
        scratch_shapes=[
            pltpu.VMEM((chan_size, FEAT, channels, channels), bf16),
            pltpu.VMEM((chan_size, channels, channels), bf16),
            pltpu.VMEM((2, 1, rows), jnp.int32),
            pltpu.VMEM((2, chan_size, rows, channels), bf16),
            pltpu.VMEM((2, 8, rows), f32),
            pltpu.VMEM((2, chan_size, 8, rows), f32),
            pltpu.VMEM((rows, channels), bf16),
            pltpu.VMEM((2, FEAT, rows, channels), f32),
            pltpu.VMEM((2, FEAT, 8, channels), f32),
            pltpu.VMEM((2, FEAT, 8, channels), f32),
            pltpu.VMEM((FEAT, rows + 8, LANES), f32),
            pltpu.VMEM((groups, rows, LANES), f32),
            pltpu.VMEM((groups, rows, LANES), f32),
            pltpu.VMEM((groups, modes, SEGS, LANES), f32),
            pltpu.VMEM((modes, channels), f32),
            pltpu.VMEM((2, seq_size, modes, channels), f32),
            pltpu.VMEM((modes, channels), f32),
            pltpu.VMEM((4, groups, modes, SEGS, LANES), f32),
            pltpu.VMEM((rows, LANES), f32),
            pltpu.VMEM((2, rows, channels), bf16),
            pltpu.VMEM((rows, channels), f32),
            pltpu.VMEM((2, 2, chan_size, rows, channels), bf16),
            pltpu.VMEM((2, 2, chan_size, rows, channels), bf16),
            pltpu.VMEM((2, rows, channels), bf16),
            pltpu.VMEM((2, rows, channels), bf16),
            dma((chan_size, FEAT)),
            dma((chan_size,)),
            dma((2,)),
            dma((2,)),
            dma((2, chan_size)),
            dma((2, chan_size)),
            dma((2, 2, chan_size)),
            dma((2, chan_size)),
            dma((2,)),
            dma((2,)),
            dma((2, 2, seq_size)),
            dma((2, 2, seq_size)),
            dma((2, 2, chan_size)),
            dma((2, 2, chan_size)),
            dma((2,)),
            dma((2,)),
        ],
        compiler_params=pltpu.CompilerParams(
            collective_id=0, has_side_effects=True, vmem_limit_bytes=60 << 20
        ),
    )(
        tokens.reshape(2, 1, rows),
        embedding,
        norm_gain.reshape(1, -1),
        short_filter,
        decay_rate,
        residue,
        skip_gain.reshape(1, channels),
        in_weight.transpose(1, 0, 2),
        out_weight,
    )


def solution(mesh):
    placed = (
        P("seq"),
        P(None, "chan"),
        P(),
        P(None, None, "chan"),
        P(None, None, "chan"),
        P(None, "chan"),
        P(None, "chan"),
        P("chan"),
        P("chan", None),
    )
    return jax.shard_map(
        functools.partial(on_device, mesh.shape["seq"], mesh.shape["chan"]),
        mesh=mesh,
        in_specs=placed,
        out_specs=P("seq", "chan"),
        check_vma=False,
    )
```

```python
import functools

import jax
import jax.numpy as jnp
from jax import lax
from jax.experimental import pallas as pl
from jax.experimental.pallas import tpu as pltpu
from jax.sharding import PartitionSpec as P

FEAT = 3
LANES = 128
SEGS = 8
MESH = pl.DeviceIdType.MESH


def block_kernel(
    seq_size,
    chan_size,
    tokens_ref,
    embed_ref,
    norm_ref,
    filter_ref,
    decay_ref,
    residue_ref,
    skip_ref,
    in_weight_ref,
    weight_ref,
    out_ref,
    in_buf,
    weight_buf,
    gathered,
    squares_out,
    squares_in,
    normed,
    proj,
    rim_out,
    rim_in,
    padded,
    query_buf,
    driven_buf,
    seg_ends,
    own_end,
    all_ends,
    incoming,
    factors,
    hidden_f,
    hidden,
    part,
    sums_out,
    sums_in,
    in_sem,
    weight_sem,
    square_send_sem,
    square_recv_sem,
    gather_send_sem,
    gather_recv_sem,
    rim_sem,
    end_send_sem,
    end_recv_sem,
    sum_send_sem,
    sum_recv_sem,
):
    place = lax.axis_index("seq")
    shard = lax.axis_index("chan")
    last = chan_size - 1
    rows = tokens_ref.shape[1]
    vocab, channels = embed_ref.shape
    modes = decay_ref.shape[0]
    groups = channels // LANES
    seg = rows // SEGS
    tile = min(256, channels)
    tiles = channels // tile

    def in_copy(d, j):
        depth = pl.ds(pl.multiple_of(d * channels, channels), channels)
        return pltpu.make_async_copy(
            in_weight_ref.at[j, depth, :], in_buf.at[d, j], in_sem.at[d, j]
        )

    def start_in(d):
        for j in range(FEAT):
            in_copy(d, j).start()

    barrier = pltpu.get_barrier_semaphore()
    for k in range(1, seq_size):
        pl.semaphore_signal(
            barrier, 1, device_id={"seq": lax.rem(place + k, seq_size)}, device_id_type=MESH
        )
    for k in range(1, chan_size):
        pl.semaphore_signal(
            barrier, 1, device_id={"chan": lax.rem(shard + k, chan_size)}, device_id_type=MESH
        )
    start_in(shard)
    for k in range(1, chan_size):
        pl.when(shard - k >= 0)(functools.partial(start_in, shard - k))
        pl.when(shard + k <= last)(functools.partial(start_in, shard + k))
    weight_copies = [
        pltpu.make_async_copy(
            weight_ref.at[:, pl.ds(d * channels, channels)], weight_buf.at[d], weight_sem.at[d]
        )
        for d in range(chan_size)
    ]
    for copy in weight_copies:
        copy.start()

    ids = lax.broadcasted_iota(jnp.int32, (vocab, rows), 0)
    one_hot = (ids == tokens_ref[...]).astype(jnp.float32).astype(jnp.bfloat16)
    stream = lax.dot_general(
        one_hot, embed_ref[...], (((0,), (0,)), ((), ())), preferred_element_type=jnp.float32
    )
    gathered[shard] = stream.astype(jnp.bfloat16)
    pl.semaphore_wait(barrier, seq_size - 1 + chan_size - 1)

    def square_copy(to, source):
        return pltpu.make_async_remote_copy(
            src_ref=squares_out,
            dst_ref=squares_in.at[source],
            send_sem=square_send_sem.at[to],
            recv_sem=square_recv_sem.at[source],
            device_id={"chan": to},
            device_id_type=MESH,
        )

    def gather_copy(way, which, to):
        return pltpu.make_async_remote_copy(
            src_ref=gathered.at[which],
            dst_ref=gathered.at[which],
            send_sem=gather_send_sem.at[way, which],
            recv_sem=gather_recv_sem.at[which],
            device_id={"chan": to},
            device_id_type=MESH,
        )

    def send_up(which):
        @pl.when(shard < last)
        def _():
            gather_copy(0, which, shard + 1).start()

    def send_down(which):
        @pl.when(shard > 0)
        def _():
            gather_copy(1, which, shard - 1).start()

    send_up(shard)
    send_down(shard)
    ones = jnp.ones((8, channels), jnp.float32)
    squares_out[...] = lax.dot_general(
        ones,
        stream * stream,
        (((1,), (1,)), ((), ())),
        precision=lax.Precision.HIGHEST,
        preferred_element_type=jnp.float32,
    )
    for k in range(1, chan_size):
        square_copy(lax.rem(shard + k, chan_size), shard).start()
    proj[...] = jnp.zeros_like(proj)
    total = squares_out[...]
    for k in range(1, chan_size):
        peer = lax.rem(shard + k, chan_size)
        square_copy(peer, shard).wait_send()
        square_copy(peer, peer).wait_recv()
        total = total + squares_in[peer]
    scale = lax.rsqrt(total.T[:, :1] * (1.0 / (channels * chan_size)) + 1e-06)

    def absorb(which):
        for j in range(FEAT):
            in_copy(which, j).wait()
        cols = pl.ds(pl.multiple_of(which * channels, channels), channels)
        normed[...] = (gathered[which].astype(jnp.float32) * scale * norm_ref[:, cols]).astype(
            jnp.bfloat16
        )

        def one(t, carry):
            j = t // tiles
            at = pl.ds(pl.multiple_of((t % tiles) * tile, tile), tile)
            proj[j, :, at] += jnp.dot(
                normed[...], in_buf[which, j, :, at], preferred_element_type=jnp.float32
            )
            return carry

        lax.fori_loop(0, FEAT * tiles, one, 0)

    absorb(shard)

    def spread(value):
        return jnp.broadcast_to(value[:, None, :], (value.shape[0], SEGS, LANES))

    def make_factors(g, carry):
        lanes = pl.ds(pl.multiple_of(g * LANES, LANES), LANES)
        decay = spread(decay_ref[:, lanes])
        left = (SEGS - 1 - lax.broadcasted_iota(jnp.int32, (1, SEGS, LANES), 1)) * seg
        factors[0, g] = jnp.exp(-decay)
        factors[1, g] = spread(residue_ref[:, lanes])
        factors[2, g] = jnp.exp(-decay * seg)
        factors[3, g] = jnp.exp(-decay * left.astype(jnp.float32))
        return carry

    def gather_step(k, carry):
        below, above = shard - k, shard + k

        @pl.when(below >= 0)
        def _():
            gather_copy(0, below, 0).wait_recv()
            send_up(below)

        @pl.when(above <= last)
        def _():
            gather_copy(1, above, 0).wait_recv()
            send_down(above)

        pl.when(below >= 0)(functools.partial(absorb, below))
        pl.when(above <= last)(functools.partial(absorb, above))

        @pl.when(k == 1)
        def _():
            lax.fori_loop(0, groups, make_factors, 0)

        return carry

    lax.fori_loop(1, chan_size, gather_step, 0)

    def rounded(value):
        return value.astype(jnp.bfloat16).astype(jnp.float32)

    for j in range(FEAT):
        rim_out[j] = rounded(proj[j, rows - 8 :, :])
    rim_copy = pltpu.make_async_remote_copy(
        src_ref=rim_out,
        dst_ref=rim_in,
        send_sem=rim_sem.at[0],
        recv_sem=rim_sem.at[1],
        device_id={"seq": lax.rem(place + 1, seq_size)},
        device_id_type=MESH,
    )
    rim_copy.start()
    keep = (place > 0).astype(jnp.float32)
    sublane = lax.broadcasted_iota(jnp.int32, (1, SEGS, LANES), 1)

    def shifted(value, by):
        return pltpu.roll(value, by, axis=1)

    def featurize(g, count, with_rim):
        lanes = pl.ds(pl.multiple_of(g * LANES, LANES), LANES)
        feat = []
        for j in range(FEAT):
            now = rounded(proj[j, :count, lanes])
            padded[j, 8 : 8 + count, :] = now
            if with_rim:
                padded[j, :8, :] = rim_in[j, :, lanes] * keep
            else:
                padded[j, :8, :] = jnp.zeros((8, LANES), jnp.float32)
            total = filter_ref[0, j : j + 1, lanes] * now
            for offset in range(1, FEAT):
                total = (
                    total
                    + filter_ref[offset, j : j + 1, lanes] * padded[j, pl.ds(8 - offset, count), :]
                )
            feat.append(rounded(total))
        query_buf[g, :count, :] = feat[0]
        driven_buf[g, :count, :] = feat[1] * feat[2]

    def feature_pass(g, carry):
        featurize(g, rows, False)
        return carry

    def first_pass(g, carry):
        lanes = pl.ds(pl.multiple_of(g * LANES, LANES), LANES)
        featurize(g, 16, True)
        lam = factors[0, g]

        def step(i, state):
            x = driven_buf[g, pl.ds(i, SEGS, stride=seg), :]
            return lam * state + x[None]

        state = lax.fori_loop(
            0, seg, step, jnp.zeros((modes, SEGS, LANES), jnp.float32), unroll=8
        )
        seg_ends[g] = state
        end = factors[3, g] * state
        for by in (4, 2, 1):
            end = end + shifted(end, by)
        end = end.reshape(modes // SEGS, SEGS, SEGS, LANES)
        mode = lax.broadcasted_iota(jnp.int32, (1, SEGS, SEGS, LANES), 1)
        row = lax.broadcasted_iota(jnp.int32, (1, SEGS, SEGS, LANES), 2)
        end = jnp.sum(jnp.where(mode == row, end, 0.0), axis=1)
        own_end[:, lanes] = end.reshape(modes, LANES)
        return carry

    halves = 2 if groups > 1 else 1
    width = channels // halves
    per_half = groups // halves

    def end_copy(half, to, source):
        cols = pl.ds(half * width, width)
        return pltpu.make_async_remote_copy(
            src_ref=own_end.at[:, cols],
            dst_ref=all_ends.at[source, :, cols],
            send_sem=end_send_sem.at[half, to],
            recv_sem=end_recv_sem.at[half, source],
            device_id={"seq": to},
            device_id_type=MESH,
        )

    for half in range(halves):
        lax.fori_loop(half * per_half, (half + 1) * per_half, feature_pass, 0)
        if half == 0:
            rim_copy.wait()
        lax.fori_loop(half * per_half, (half + 1) * per_half, first_pass, 0)
        for k in range(1, seq_size):
            end_copy(half, lax.rem(place + k, seq_size), place).start()
    all_ends[place] = own_end[...]

    def second_pass(g, carry):
        lanes = pl.ds(pl.multiple_of(g * LANES, LANES), LANES)
        start = jnp.where(sublane > 0, shifted(seg_ends[g], 1), spread(incoming[:, lanes]))
        power = factors[2, g]
        for by in (1, 2, 4):
            start = start + jnp.where(sublane >= by, power * shifted(start, by), 0.0)
            power = power * power
        lam = factors[0, g]
        gain = factors[1, g]
        skip = jnp.broadcast_to(skip_ref[:, lanes], (SEGS, LANES))

        def step(i, state):
            at = pl.ds(i, SEGS, stride=seg)
            x = driven_buf[g, at, :]
            state = lam * state + x[None]
            long = jnp.sum(gain * state, axis=0) + skip * x
            hidden_f[at, :] = query_buf[g, at, :] * long
            return state

        lax.fori_loop(0, seg, step, start, unroll=8)
        hidden[:, lanes] = hidden_f[...].astype(jnp.bfloat16)
        return carry

    for half in range(halves):
        for k in range(1, seq_size):
            peer = lax.rem(place + k, seq_size)
            end_copy(half, peer, place).wait_send()
            end_copy(half, peer, peer).wait_recv()
        cols = slice(half * width, (half + 1) * width)
        span = jnp.exp(-decay_ref[:, cols] * rows)
        state = jnp.zeros((modes, width), jnp.float32)
        for p in range(seq_size - 1):
            state = jnp.where(p < place, span * state + all_ends[p, :, cols], state)
        incoming[:, cols] = state
        lax.fori_loop(half * per_half, (half + 1) * per_half, second_pass, 0)
    for copy in weight_copies:
        copy.wait()

    def project(dest):
        def one(t, carry):
            cols = pl.ds(pl.multiple_of(t * tile, tile), tile)
            part[:, cols] = jnp.dot(
                hidden[...], weight_buf[dest, :, cols], preferred_element_type=jnp.float32
            )
            return carry

        lax.fori_loop(0, tiles, one, 0)

    def sum_copy(way, dest, to):
        return pltpu.make_async_remote_copy(
            src_ref=sums_out.at[way, dest],
            dst_ref=sums_in.at[way, dest],
            send_sem=sum_send_sem.at[way, dest],
            recv_sem=sum_recv_sem.at[way, dest],
            device_id={"chan": to},
            device_id_type=MESH,
        )

    def pass_on(way, dest, to, has_earlier):
        project(dest)

        @pl.when(has_earlier)
        def _():
            sum_copy(way, dest, to).wait_recv()
            sums_out[way, dest] = (part[...] + sums_in[way, dest].astype(jnp.float32)).astype(
                jnp.bfloat16
            )

        @pl.when(jnp.logical_not(has_earlier))
        def _():
            sums_out[way, dest] = part[...].astype(jnp.bfloat16)

        sum_copy(way, dest, to).start()

    def sum_step(t, carry):
        up = last - (t - shard)

        @pl.when((t >= shard) & (up > shard))
        def _():
            pass_on(0, up, shard + 1, shard > 0)

        down = t - (last - shard)

        @pl.when((down >= 0) & (down < shard))
        def _():
            pass_on(1, down, shard - 1, shard < last)

        return carry

    lax.fori_loop(0, 2 * last, sum_step, 0)

    project(shard)
    part[...] += gathered[shard].astype(jnp.float32)

    @pl.when(shard > 0)
    def _():
        sum_copy(0, shard, 0).wait_recv()
        part[...] += sums_in[0, shard].astype(jnp.float32)

    @pl.when(shard < last)
    def _():
        sum_copy(1, shard, 0).wait_recv()
        part[...] += sums_in[1, shard].astype(jnp.float32)

    out_ref[...] = part[...].astype(jnp.bfloat16)

    def drain(dest, carry):
        @pl.when(dest > shard)
        def _():
            sum_copy(0, dest, 0).wait_send()

        @pl.when(dest < shard)
        def _():
            sum_copy(1, dest, 0).wait_send()

        @pl.when((dest <= shard) & (shard < last))
        def _():
            gather_copy(0, dest, 0).wait_send()

        @pl.when((dest >= shard) & (shard > 0))
        def _():
            gather_copy(1, dest, 0).wait_send()

        return carry

    lax.fori_loop(0, chan_size, drain, 0)


def on_device(
    seq_size,
    chan_size,
    tokens,
    embedding,
    norm_gain,
    in_weight,
    short_filter,
    decay_rate,
    residue,
    skip_gain,
    out_weight,
):
    rows = tokens.shape[0]
    channels = embedding.shape[1]
    modes = decay_rate.shape[0]
    groups = channels // LANES
    f32, bf16 = jnp.float32, jnp.bfloat16
    vmem = pl.BlockSpec(memory_space=pltpu.VMEM)
    hbm = pl.BlockSpec(memory_space=pl.ANY)
    dma = pltpu.SemaphoreType.DMA
    return pl.pallas_call(
        functools.partial(block_kernel, seq_size, chan_size),
        out_shape=jax.ShapeDtypeStruct((rows, channels), bf16),
        in_specs=[vmem] * 7 + [hbm] * 2,
        out_specs=vmem,
        scratch_shapes=[
            pltpu.VMEM((chan_size, FEAT, channels, channels), bf16),
            pltpu.VMEM((chan_size, channels, channels), bf16),
            pltpu.VMEM((chan_size, rows, channels), bf16),
            pltpu.VMEM((8, rows), f32),
            pltpu.VMEM((chan_size, 8, rows), f32),
            pltpu.VMEM((rows, channels), bf16),
            pltpu.VMEM((FEAT, rows, channels), f32),
            pltpu.VMEM((FEAT, 8, channels), f32),
            pltpu.VMEM((FEAT, 8, channels), f32),
            pltpu.VMEM((FEAT, rows + 8, LANES), f32),
            pltpu.VMEM((groups, rows, LANES), f32),
            pltpu.VMEM((groups, rows, LANES), f32),
            pltpu.VMEM((groups, modes, SEGS, LANES), f32),
            pltpu.VMEM((modes, channels), f32),
            pltpu.VMEM((seq_size, modes, channels), f32),
            pltpu.VMEM((modes, channels), f32),
            pltpu.VMEM((4, groups, modes, SEGS, LANES), f32),
            pltpu.VMEM((rows, LANES), f32),
            pltpu.VMEM((rows, channels), bf16),
            pltpu.VMEM((rows, channels), f32),
            pltpu.VMEM((2, chan_size, rows, channels), bf16),
            pltpu.VMEM((2, chan_size, rows, channels), bf16),
            dma((chan_size, FEAT)),
            dma((chan_size,)),
            dma((chan_size,)),
            dma((chan_size,)),
            dma((2, chan_size)),
            dma((chan_size,)),
            dma((2,)),
            dma((2, seq_size)),
            dma((2, seq_size)),
            dma((2, chan_size)),
            dma((2, chan_size)),
        ],
        compiler_params=pltpu.CompilerParams(
            collective_id=0, has_side_effects=True, vmem_limit_bytes=60 << 20
        ),
    )(
        tokens.reshape(1, rows),
        embedding,
        norm_gain.reshape(1, -1),
        short_filter,
        decay_rate,
        residue,
        skip_gain.reshape(1, channels),
        in_weight.transpose(1, 0, 2),
        out_weight,
    )


def solution(mesh):
    placed = (
        P("seq"),
        P(None, "chan"),
        P(),
        P(None, None, "chan"),
        P(None, None, "chan"),
        P(None, "chan"),
        P(None, "chan"),
        P("chan"),
        P("chan", None),
    )
    return jax.shard_map(
        functools.partial(on_device, mesh.shape["seq"], mesh.shape["chan"]),
        mesh=mesh,
        in_specs=placed,
        out_specs=P("seq", "chan"),
        check_vma=False,
    )
```

```python
import functools

import jax
import jax.numpy as jnp
from jax import lax
from jax.experimental import pallas as pl
from jax.experimental.pallas import tpu as pltpu
from jax.sharding import PartitionSpec as P

FEAT = 3
LANES = 128
SEGS = 8
MESH = pl.DeviceIdType.MESH


def block_kernel(
    seq_size,
    chan_size,
    tokens_ref,
    embed_ref,
    norm_ref,
    filter_ref,
    decay_ref,
    residue_ref,
    skip_ref,
    in_weight_ref,
    weight_ref,
    out_ref,
    in_buf,
    weight_buf,
    gathered,
    squares_out,
    squares_in,
    normed,
    proj,
    rim_out,
    rim_in,
    padded,
    query_buf,
    driven_buf,
    seg_ends,
    own_end,
    all_ends,
    incoming,
    factors,
    hidden_f,
    hidden,
    part,
    sums_in,
    in_sem,
    weight_sem,
    square_send_sem,
    square_recv_sem,
    gather_send_sem,
    gather_recv_sem,
    rim_sem,
    end_send_sem,
    end_recv_sem,
    sum_send_sem,
    sum_recv_sem,
):
    place = lax.axis_index("seq")
    shard = lax.axis_index("chan")
    last = chan_size - 1
    rows = tokens_ref.shape[1]
    vocab, channels = embed_ref.shape
    modes = decay_ref.shape[0]
    groups = channels // LANES
    seg = rows // SEGS
    tile = min(512, channels)
    tiles = channels // tile

    def in_copy(d, j):
        depth = pl.ds(pl.multiple_of(d * channels, channels), channels)
        return pltpu.make_async_copy(
            in_weight_ref.at[j, depth, :], in_buf.at[d, j], in_sem.at[d, j]
        )

    def start_in(d):
        for j in range(FEAT):
            in_copy(d, j).start()

    barrier = pltpu.get_barrier_semaphore()
    for k in range(1, seq_size):
        pl.semaphore_signal(
            barrier, 1, device_id={"seq": lax.rem(place + k, seq_size)}, device_id_type=MESH
        )
    for k in range(1, chan_size):
        pl.semaphore_signal(
            barrier, 1, device_id={"chan": lax.rem(shard + k, chan_size)}, device_id_type=MESH
        )
    start_in(shard)
    for k in range(1, chan_size):
        pl.when(shard - k >= 0)(functools.partial(start_in, shard - k))
        pl.when(shard + k <= last)(functools.partial(start_in, shard + k))
    weight_copies = [
        pltpu.make_async_copy(
            weight_ref.at[:, pl.ds(d * channels, channels)], weight_buf.at[d], weight_sem.at[d]
        )
        for d in range(chan_size)
    ]
    for copy in weight_copies:
        copy.start()

    ids = lax.broadcasted_iota(jnp.int32, (vocab, rows), 0)
    one_hot = (ids == tokens_ref[...]).astype(jnp.float32).astype(jnp.bfloat16)
    stream = lax.dot_general(
        one_hot, embed_ref[...], (((0,), (0,)), ((), ())), preferred_element_type=jnp.float32
    )
    gathered[shard] = stream.astype(jnp.bfloat16)
    ones = jnp.ones((8, channels), jnp.float32)
    squares_out[...] = lax.dot_general(
        ones,
        stream * stream,
        (((1,), (1,)), ((), ())),
        precision=lax.Precision.HIGHEST,
        preferred_element_type=jnp.float32,
    )
    pl.semaphore_wait(barrier, seq_size - 1 + chan_size - 1)

    def square_copy(to, source):
        return pltpu.make_async_remote_copy(
            src_ref=squares_out,
            dst_ref=squares_in.at[source],
            send_sem=square_send_sem.at[to],
            recv_sem=square_recv_sem.at[source],
            device_id={"chan": to},
            device_id_type=MESH,
        )

    def gather_copy(way, which, to):
        return pltpu.make_async_remote_copy(
            src_ref=gathered.at[which],
            dst_ref=gathered.at[which],
            send_sem=gather_send_sem.at[way, which],
            recv_sem=gather_recv_sem.at[which],
            device_id={"chan": to},
            device_id_type=MESH,
        )

    def send_up(which):
        @pl.when(shard < last)
        def _():
            gather_copy(0, which, shard + 1).start()

    def send_down(which):
        @pl.when(shard > 0)
        def _():
            gather_copy(1, which, shard - 1).start()

    for k in range(1, chan_size):
        square_copy(lax.rem(shard + k, chan_size), shard).start()
    send_up(shard)
    send_down(shard)
    proj[...] = jnp.zeros_like(proj)
    total = squares_out[...]
    for k in range(1, chan_size):
        peer = lax.rem(shard + k, chan_size)
        square_copy(peer, shard).wait_send()
        square_copy(peer, peer).wait_recv()
        total = total + squares_in[peer]
    scale = lax.rsqrt(total.T[:, :1] * (1.0 / (channels * chan_size)) + 1e-06)

    def absorb(which):
        for j in range(FEAT):
            in_copy(which, j).wait()
        cols = pl.ds(pl.multiple_of(which * channels, channels), channels)
        normed[...] = (gathered[which].astype(jnp.float32) * scale * norm_ref[:, cols]).astype(
            jnp.bfloat16
        )

        def one(t, carry):
            j = t // tiles
            at = pl.ds(pl.multiple_of((t % tiles) * tile, tile), tile)
            proj[j, :, at] += jnp.dot(
                normed[...], in_buf[which, j, :, at], preferred_element_type=jnp.float32
            )
            return carry

        lax.fori_loop(0, FEAT * tiles, one, 0)

    absorb(shard)

    def spread(value):
        return jnp.broadcast_to(value[:, None, :], (value.shape[0], SEGS, LANES))

    def make_factors(g, carry):
        lanes = pl.ds(pl.multiple_of(g * LANES, LANES), LANES)
        decay = spread(decay_ref[:, lanes])
        left = (SEGS - 1 - lax.broadcasted_iota(jnp.int32, (1, SEGS, LANES), 1)) * seg
        factors[0, g] = jnp.exp(-decay)
        factors[1, g] = spread(residue_ref[:, lanes])
        factors[2, g] = jnp.exp(-decay * seg)
        factors[3, g] = jnp.exp(-decay * left.astype(jnp.float32))
        return carry

    def gather_step(k, carry):
        below, above = shard - k, shard + k

        @pl.when(below >= 0)
        def _():
            gather_copy(0, below, 0).wait_recv()
            send_up(below)

        @pl.when(above <= last)
        def _():
            gather_copy(1, above, 0).wait_recv()
            send_down(above)

        pl.when(below >= 0)(functools.partial(absorb, below))
        pl.when(above <= last)(functools.partial(absorb, above))

        @pl.when(k == 1)
        def _():
            lax.fori_loop(0, groups, make_factors, 0)

        return carry

    lax.fori_loop(1, chan_size, gather_step, 0)

    def rounded(value):
        return value.astype(jnp.bfloat16).astype(jnp.float32)

    for j in range(FEAT):
        rim_out[j] = rounded(proj[j, rows - 8 :, :])
    rim_copy = pltpu.make_async_remote_copy(
        src_ref=rim_out,
        dst_ref=rim_in,
        send_sem=rim_sem.at[0],
        recv_sem=rim_sem.at[1],
        device_id={"seq": lax.rem(place + 1, seq_size)},
        device_id_type=MESH,
    )
    rim_copy.start()
    keep = (place > 0).astype(jnp.float32)
    sublane = lax.broadcasted_iota(jnp.int32, (1, SEGS, LANES), 1)

    def shifted(value, by):
        return pltpu.roll(value, by, axis=1)

    def featurize(g, count, with_rim):
        lanes = pl.ds(pl.multiple_of(g * LANES, LANES), LANES)
        feat = []
        for j in range(FEAT):
            now = rounded(proj[j, :count, lanes])
            padded[j, 8 : 8 + count, :] = now
            if with_rim:
                padded[j, :8, :] = rim_in[j, :, lanes] * keep
            else:
                padded[j, :8, :] = jnp.zeros((8, LANES), jnp.float32)
            total = filter_ref[0, j : j + 1, lanes] * now
            for offset in range(1, FEAT):
                total = (
                    total
                    + filter_ref[offset, j : j + 1, lanes] * padded[j, pl.ds(8 - offset, count), :]
                )
            feat.append(rounded(total))
        query_buf[g, :count, :] = feat[0]
        driven_buf[g, :count, :] = feat[1] * feat[2]

    def feature_pass(g, carry):
        featurize(g, rows, False)
        return carry

    def first_pass(g, carry):
        lanes = pl.ds(pl.multiple_of(g * LANES, LANES), LANES)
        featurize(g, 16, True)
        lam = factors[0, g]

        def step(i, state):
            x = driven_buf[g, pl.ds(i, SEGS, stride=seg), :]
            return lam * state + x[None]

        state = lax.fori_loop(
            0, seg, step, jnp.zeros((modes, SEGS, LANES), jnp.float32), unroll=8
        )
        seg_ends[g] = state
        end = factors[3, g] * state
        for by in (4, 2, 1):
            end = end + shifted(end, by)
        end = end.reshape(modes // SEGS, SEGS, SEGS, LANES)
        mode = lax.broadcasted_iota(jnp.int32, (1, SEGS, SEGS, LANES), 1)
        row = lax.broadcasted_iota(jnp.int32, (1, SEGS, SEGS, LANES), 2)
        end = jnp.sum(jnp.where(mode == row, end, 0.0), axis=1)
        own_end[:, lanes] = end.reshape(modes, LANES)
        return carry

    halves = 2 if groups > 1 else 1
    width = channels // halves
    per_half = groups // halves

    def end_copy(half, to, source):
        cols = pl.ds(half * width, width)
        return pltpu.make_async_remote_copy(
            src_ref=own_end.at[:, cols],
            dst_ref=all_ends.at[source, :, cols],
            send_sem=end_send_sem.at[half, to],
            recv_sem=end_recv_sem.at[half, source],
            device_id={"seq": to},
            device_id_type=MESH,
        )

    for half in range(halves):
        lax.fori_loop(half * per_half, (half + 1) * per_half, feature_pass, 0)
        if half == 0:
            rim_copy.wait()
        lax.fori_loop(half * per_half, (half + 1) * per_half, first_pass, 0)
        for k in range(1, seq_size):
            end_copy(half, lax.rem(place + k, seq_size), place).start()
    all_ends[place] = own_end[...]

    def second_pass(g, carry):
        lanes = pl.ds(pl.multiple_of(g * LANES, LANES), LANES)
        start = jnp.where(sublane > 0, shifted(seg_ends[g], 1), spread(incoming[:, lanes]))
        power = factors[2, g]
        for by in (1, 2, 4):
            start = start + jnp.where(sublane >= by, power * shifted(start, by), 0.0)
            power = power * power
        lam = factors[0, g]
        gain = factors[1, g]
        skip = jnp.broadcast_to(skip_ref[:, lanes], (SEGS, LANES))

        def step(i, state):
            at = pl.ds(i, SEGS, stride=seg)
            x = driven_buf[g, at, :]
            state = lam * state + x[None]
            long = jnp.sum(gain * state, axis=0) + skip * x
            hidden_f[at, :] = query_buf[g, at, :] * long
            return state

        lax.fori_loop(0, seg, step, start, unroll=8)
        hidden[:, lanes] = hidden_f[...].astype(jnp.bfloat16)
        return carry

    for half in range(halves):
        for k in range(1, seq_size):
            peer = lax.rem(place + k, seq_size)
            end_copy(half, peer, place).wait_send()
            end_copy(half, peer, peer).wait_recv()
        cols = slice(half * width, (half + 1) * width)
        span = jnp.exp(-decay_ref[:, cols] * rows)
        state = jnp.zeros((modes, width), jnp.float32)
        for p in range(seq_size - 1):
            state = jnp.where(p < place, span * state + all_ends[p, :, cols], state)
        incoming[:, cols] = state
        lax.fori_loop(half * per_half, (half + 1) * per_half, second_pass, 0)
    for copy in weight_copies:
        copy.wait()

    def project(dest):
        def one(t, carry):
            cols = pl.ds(pl.multiple_of(t * tile, tile), tile)
            part[:, cols] = jnp.dot(
                hidden[...], weight_buf[dest, :, cols], preferred_element_type=jnp.float32
            )
            return carry

        lax.fori_loop(0, tiles, one, 0)

    def sum_copy(way, dest, to):
        return pltpu.make_async_remote_copy(
            src_ref=in_buf.at[dest, way, pl.ds(0, rows), :],
            dst_ref=sums_in.at[way, dest],
            send_sem=sum_send_sem.at[way, dest],
            recv_sem=sum_recv_sem.at[way, dest],
            device_id={"chan": to},
            device_id_type=MESH,
        )

    def pass_on(way, dest, to, has_earlier):
        project(dest)

        @pl.when(has_earlier)
        def _():
            sum_copy(way, dest, to).wait_recv()
            in_buf[dest, way, :rows, :] = (part[...] + sums_in[way, dest].astype(jnp.float32)).astype(
                jnp.bfloat16
            )

        @pl.when(jnp.logical_not(has_earlier))
        def _():
            in_buf[dest, way, :rows, :] = part[...].astype(jnp.bfloat16)

        sum_copy(way, dest, to).start()

    def sum_step(t, carry):
        up = last - (t - shard)

        @pl.when((t >= shard) & (up > shard))
        def _():
            pass_on(0, up, shard + 1, shard > 0)

        down = t - (last - shard)

        @pl.when((down >= 0) & (down < shard))
        def _():
            pass_on(1, down, shard - 1, shard < last)

        return carry

    lax.fori_loop(0, 2 * last, sum_step, 0)

    project(shard)
    part[...] += gathered[shard].astype(jnp.float32)

    @pl.when(shard > 0)
    def _():
        sum_copy(0, shard, 0).wait_recv()
        part[...] += sums_in[0, shard].astype(jnp.float32)

    @pl.when(shard < last)
    def _():
        sum_copy(1, shard, 0).wait_recv()
        part[...] += sums_in[1, shard].astype(jnp.float32)

    out_ref[...] = part[...].astype(jnp.bfloat16)

    def drain(dest, carry):
        @pl.when(dest > shard)
        def _():
            sum_copy(0, dest, 0).wait_send()

        @pl.when(dest < shard)
        def _():
            sum_copy(1, dest, 0).wait_send()

        @pl.when((dest <= shard) & (shard < last))
        def _():
            gather_copy(0, dest, 0).wait_send()

        @pl.when((dest >= shard) & (shard > 0))
        def _():
            gather_copy(1, dest, 0).wait_send()

        return carry

    lax.fori_loop(0, chan_size, drain, 0)


def on_device(
    seq_size,
    chan_size,
    tokens,
    embedding,
    norm_gain,
    in_weight,
    short_filter,
    decay_rate,
    residue,
    skip_gain,
    out_weight,
):
    rows = tokens.shape[0]
    channels = embedding.shape[1]
    modes = decay_rate.shape[0]
    groups = channels // LANES
    f32, bf16 = jnp.float32, jnp.bfloat16
    vmem = pl.BlockSpec(memory_space=pltpu.VMEM)
    hbm = pl.BlockSpec(memory_space=pl.ANY)
    dma = pltpu.SemaphoreType.DMA
    return pl.pallas_call(
        functools.partial(block_kernel, seq_size, chan_size),
        out_shape=jax.ShapeDtypeStruct((rows, channels), bf16),
        in_specs=[vmem] * 7 + [hbm] * 2,
        out_specs=vmem,
        scratch_shapes=[
            pltpu.VMEM((chan_size, FEAT, channels, channels), bf16),
            pltpu.VMEM((chan_size, channels, channels), bf16),
            pltpu.VMEM((chan_size, rows, channels), bf16),
            pltpu.VMEM((8, rows), f32),
            pltpu.VMEM((chan_size, 8, rows), f32),
            pltpu.VMEM((rows, channels), bf16),
            pltpu.VMEM((FEAT, rows, channels), f32),
            pltpu.VMEM((FEAT, 8, channels), f32),
            pltpu.VMEM((FEAT, 8, channels), f32),
            pltpu.VMEM((FEAT, rows + 8, LANES), f32),
            pltpu.VMEM((groups, rows, LANES), f32),
            pltpu.VMEM((groups, rows, LANES), f32),
            pltpu.VMEM((groups, modes, SEGS, LANES), f32),
            pltpu.VMEM((modes, channels), f32),
            pltpu.VMEM((seq_size, modes, channels), f32),
            pltpu.VMEM((modes, channels), f32),
            pltpu.VMEM((4, groups, modes, SEGS, LANES), f32),
            pltpu.VMEM((rows, LANES), f32),
            pltpu.VMEM((rows, channels), bf16),
            pltpu.VMEM((rows, channels), f32),
            pltpu.VMEM((2, chan_size, rows, channels), bf16),
            dma((chan_size, FEAT)),
            dma((chan_size,)),
            dma((chan_size,)),
            dma((chan_size,)),
            dma((2, chan_size)),
            dma((chan_size,)),
            dma((2,)),
            dma((2, seq_size)),
            dma((2, seq_size)),
            dma((2, chan_size)),
            dma((2, chan_size)),
        ],
        compiler_params=pltpu.CompilerParams(
            collective_id=0, has_side_effects=True, vmem_limit_bytes=54 << 20
        ),
    )(
        tokens.reshape(1, rows),
        embedding,
        norm_gain.reshape(1, -1),
        short_filter,
        decay_rate,
        residue,
        skip_gain.reshape(1, channels),
        in_weight.transpose(1, 0, 2),
        out_weight,
    )


def solution(mesh):
    placed = (
        P("seq"),
        P(None, "chan"),
        P(),
        P(None, None, "chan"),
        P(None, None, "chan"),
        P(None, "chan"),
        P(None, "chan"),
        P("chan"),
        P("chan", None),
    )
    return jax.shard_map(
        functools.partial(on_device, mesh.shape["seq"], mesh.shape["chan"]),
        mesh=mesh,
        in_specs=placed,
        out_specs=P("seq", "chan"),
        check_vma=False,
    )
```
